32 devices in a mesh: dp: 16 (over z, x, core), fsdp: 2 (over y).
Axes of the slice: x: 2, y: 2, z: 4, core: 2. Of those that a mesh axis runs over, the one named last changes fastest.
Arguments:
- attn: bfloat16 [18432, 1536], P(('dp', 'fsdp')), may hold values from -6 to 6
- cotangent: bfloat16 [18432, 3072], P(('dp', 'fsdp')), may hold values from -12 to 12
- weight: bfloat16 [1536, 3072], P('fsdp'), may hold values from -0.15625 to 0.15625
- projector: bfloat16 [1536, 256], replicated, may hold values from -0.15625 to 0.15625
- moment_one: float32 [3072, 256], P(('dp', 'fsdp')), may hold values from -256 to 256
- moment_two: float32 [3072, 256], P(('dp', 'fsdp')), may hold values from 30 to 3000
- step_count: int32 [1], replicated, may hold values from 1 to 10
Outputs:
- grad_input: bfloat16 [18432, 1536], P(('dp', 'fsdp'))
- weight_step: float32 [1536, 3072], P('fsdp')
- first_moment: float32 [3072, 256], P(('dp', 'fsdp'))
- second_moment: float32 [3072, 256], P(('dp', 'fsdp'))
The draws below stay inside these ranges and needn't reach their ends.
All inputs are finite; a program needn't handle non-finite values.
Results may differ from the reference program's by a relative error of at most 0.015.
Values may be sent and summed in bfloat16 or wider, within the bound.
No kernel may reach another device: no remote copies, remote signals or barrier semaphores. Data moves between devices by JAX's collectives and lax.ppermute only.
A program may use at most 128 MiB of HBM per device.

```python
import math
import jax
import jax.numpy as jnp
from jax import lax

D = 3072
DI = 1536
R = 256
TOKENS = 18432


def raised(array, rng, source, target, blocks, factor):
    def block_of(position):
        return (jnp.arange(array.shape[position]) // (array.shape[position] // blocks)).reshape((-1,) + (1,) * (array.ndim - 1 - position))

    near = jax.random.permutation(rng, blocks)[block_of(target)]
    second = (block_of(target) + blocks // 2) % blocks
    return jnp.where((block_of(source) == near) | (block_of(source) == second), factor * array, array)


def level_of(stream_key, extent, split, smallest, largest):
    loudness = 1.0
    for position, shards_of in split:
        steps = jax.random.uniform(jax.random.fold_in(jax.random.fold_in(stream_key, 6), position), (shards_of,), jnp.float32, smallest / len(split), largest / len(split))
        loudness = loudness * jnp.repeat(jnp.exp(steps), extent[position] // shards_of).reshape((-1,) + (1,) * (len(extent) - 1 - position))
    return loudness


def gaussian(key, shape, spread, limit, split=(), held_as=jnp.bfloat16):
    entries = jax.random.normal(key, shape, jnp.float32) * spread
    if len(split) > 0:
        entries = level_of(key, shape, split, -0.22, 0.18) * entries
    return jnp.clip(entries, min=-limit, max=limit).astype(held_as)


def bell_draw_with(key, extent, width, most, split, heavy, held_as=jnp.bfloat16):
    array = width * jax.random.normal(key, extent, jnp.float32)
    if split:
        array = array * level_of(key, extent, split, -0.22, 0.18)
    return jnp.clip(raised(array, jax.random.fold_in(key, 3), *heavy), -most, most).astype(held_as)


def setup_inputs(seed: int = 0) -> dict:
    splits = jax.random.split(jax.random.key(seed), 8)
    attn = gaussian(splits[0], (TOKENS, DI), 1.0, 6.0, ((0, 32),))
    cotangent = bell_draw_with(splits[1], (TOKENS, D), 1.0, 12.0, ((0, 32),), (0, 1, 32, 2.75))
    weight = gaussian(splits[2], (DI, D), DI ** -0.5, 0.15625, ((0, 2),))
    projector = gaussian(splits[3], (DI, R), DI ** -0.5, 0.15625)
    moment_one = gaussian(splits[4], (D, R), 40.0, 256.0, ((0, 32),), jnp.float32)
    moment_two = jnp.clip(jnp.exp(math.log(3000.0) - 4.6051702 * jax.random.uniform(splits[5], (D, R), jnp.float32) ** level_of(splits[5], (D, R), ((0, 32),), -0.2, 0.2)), 30.0, 3000.0)
    step_count = jax.random.randint(splits[6], (1,), 1, 11).astype(jnp.int32)
    return {"attn": attn, "cotangent": cotangent, "weight": weight, "projector": projector, "moment_one": moment_one, "moment_two": moment_two, "step_count": step_count}


def reference(attn, cotangent, weight, projector, moment_one, moment_two, step_count):
    reduced = jnp.dot(attn, projector, preferred_element_type=jnp.float32).astype(jnp.bfloat16)
    grad_input = lax.dot_general(cotangent, weight, (((1,), (1,)), ((), ())), preferred_element_type=jnp.float32).astype(jnp.bfloat16)
    projected = lax.dot_general(cotangent, reduced, (((0,), (0,)), ((), ())), preferred_element_type=jnp.float32)
    first_moment = 0.9 * moment_one + 0.1 * projected
    second_moment = 0.999 * moment_two + 0.001 * projected * projected
    steps = step_count[0].astype(jnp.float32)
    first_hat = first_moment / (1.0 - jnp.power(jnp.float32(0.9), steps))
    second_hat = second_moment / (1.0 - jnp.power(jnp.float32(0.999), steps))
    low_step = (first_hat / (jnp.sqrt(second_hat) + 1e-08)).astype(jnp.bfloat16)
    weight_step = 0.25 * lax.dot_general(projector, low_step, (((1,), (1,)), ((), ())), preferred_element_type=jnp.float32)
    return (grad_input, weight_step, first_moment, second_moment)
```

```python
import jax
import jax.numpy as jnp
from jax import lax
from jax.sharding import PartitionSpec as P

AXES = ("dp", "fsdp")


def solution(mesh):
    n_dp, n_y = mesh.shape["dp"], mesh.shape["fsdp"]
    n_z = n_dp // 4

    def send(value, move):
        pairs = []
        for z in range(n_z):
            for x in range(2):
                for c in range(2):
                    for y in range(n_y):
                        tz, tx, tc, ty = move(z, x, c, y)
                        pairs.append(
                            (((z * 2 + x) * 2 + c) * n_y + y, ((tz * 2 + tx) * 2 + tc) * n_y + ty)
                        )
        return lax.ppermute(value, AXES, pairs)

    def to_core(value):
        return send(value, lambda z, x, c, y: (z, x, 1 - c, y))

    def to_plane(value, dx, dy):
        return send(value, lambda z, x, c, y: (z, x ^ dx, c, (y + dy) % n_y))

    def to_z(value, dz):
        return send(value, lambda z, x, c, y: ((z + dz) % n_z, x, c, y))

    def to_z_pair(value):
        return send(value, lambda z, x, c, y: (z ^ 1, x, c, y))

    plane = [(dx, dy) for dx in range(2) for dy in range(n_y) if (dx, dy) != (0, 0)]

    def on_device(attn, cotangent, weight, projector, moment_one, moment_two, step_count):
        d, y = lax.axis_index("dp"), lax.axis_index("fsdp")
        c, x, z = d % 2, (d // 2) % 2, d // 4
        shard_rows, width = weight.shape
        own_rows, rank = moment_one.shape
        f32, bf16 = jnp.float32, jnp.bfloat16

        def weight_piece(q):
            return lax.dynamic_index_in_dim(
                weight.reshape(8, shard_rows // 8, width), q, 0, keepdims=False
            )

        q = (x * 2 + z % 2) * 2 + c
        shards = []
        for dy in range(1, n_y):
            own = to_plane(weight_piece(q), 0, dy)
            over_x, over_z = to_plane(own, 1, 0), to_z_pair(own)
            half = own.shape[0] // 2
            low, high = to_plane(over_z[:half], 1, 0), to_z_pair(over_x[half:])
            mine = [own, over_z, over_x, jnp.concatenate([low, high])]
            theirs = [to_core(piece) for piece in mine]
            full = jnp.zeros((8, shard_rows // 8, width), bf16)
            for k in range(4):
                qk = q ^ (2 * k)
                full = lax.dynamic_update_index_in_dim(full, mine[k], qk, 0)
                full = lax.dynamic_update_index_in_dim(full, theirs[k], qk ^ 1, 0)
            shards.append(full.reshape(shard_rows, width))

        reduced = jnp.dot(attn, projector, preferred_element_type=f32).astype(bf16)
        partial = lax.dot_general(
            cotangent, reduced, (((0,), (0,)), ((), ())), preferred_element_type=f32
        ).reshape(n_z, 2, 2, n_y, own_rows, rank)
        got = to_core(lax.dynamic_index_in_dim(partial, 1 - c, 2, keepdims=False).astype(bf16))
        chip = lax.dynamic_index_in_dim(partial, c, 2, keepdims=False) + got.astype(f32)

        def plane_part(tx, ty):
            part = lax.dynamic_index_in_dim(chip, tx, 1, keepdims=False)
            return lax.dynamic_index_in_dim(part, ty, 1, keepdims=False)

        total = plane_part(x, y)
        for dx, dy in plane:
            got = to_plane(plane_part(x ^ dx, (y + dy) % n_y).astype(bf16), dx, dy)
            total = total + got.astype(f32)
        projected = lax.dynamic_index_in_dim(total, z, 0, keepdims=False)
        for dz in range(1, n_z):
            part = lax.dynamic_index_in_dim(total, (z + dz) % n_z, 0, keepdims=False)
            projected = projected + to_z(part.astype(bf16), dz).astype(f32)

        first_moment = 0.9 * moment_one + 0.1 * projected
        second_moment = 0.999 * moment_two + 0.001 * projected * projected
        steps = step_count[0].astype(f32)
        first_hat = first_moment / (1.0 - jnp.power(f32(0.9), steps))
        second_hat = second_moment / (1.0 - jnp.power(f32(0.999), steps))
        low_step = (first_hat / (jnp.sqrt(second_hat) + 1e-08)).astype(bf16)

        column = jnp.zeros((n_z, own_rows, rank), bf16)
        column = lax.dynamic_update_index_in_dim(column, low_step, z, 0)
        for dz in range(1, n_z):
            column = lax.dynamic_update_index_in_dim(
                column, to_z(low_step, dz), (z - dz) % n_z, 0
            )
        whole = jnp.zeros((2, 2, n_y, n_z, own_rows, rank), bf16)

        def place(whole, block, px, pc, py):
            return lax.dynamic_update_slice(whole, block[None, None, None], (pc, px, py, 0, 0, 0))

        whole = place(whole, column, x, c, y)
        whole = place(whole, to_core(column), x, 1 - c, y)
        for dx, dy in plane:
            got = to_plane(column, dx, dy)
            whole = place(whole, got, x ^ dx, c, (y - dy) % n_y)
            whole = place(whole, to_core(got), x ^ dx, 1 - c, (y - dy) % n_y)
        low_full = whole.transpose(3, 1, 0, 2, 4, 5).reshape(-1, rank)

        my_projector = lax.dynamic_slice_in_dim(projector, y * shard_rows, shard_rows, 0)
        weight_step = 0.25 * lax.dot_general(
            my_projector, low_full, (((1,), (1,)), ((), ())), preferred_element_type=f32
        )

        def columns_of(rows):
            return lax.dot_general(
                cotangent, rows, (((1,), (1,)), ((), ())), preferred_element_type=f32
            ).astype(bf16)

        grad_input = jnp.zeros((attn.shape[0], shard_rows * n_y), bf16)
        grad_input = lax.dynamic_update_slice_in_dim(
            grad_input, columns_of(weight), y * shard_rows, 1
        )
        for dy in range(1, n_y):
            grad_input = lax.dynamic_update_slice_in_dim(
                grad_input, columns_of(shards[dy - 1]), ((y - dy) % n_y) * shard_rows, 1
            )
        return grad_input, weight_step, first_moment, second_moment

    rows = P(("dp", "fsdp"), None)
    return jax.shard_map(
        on_device,
        mesh=mesh,
        in_specs=(rows, rows, P("fsdp", None), P(), rows, rows, P()),
        out_specs=(rows, P("fsdp", None), rows, rows),
        check_vma=False,
    )
```

```python
import jax
import jax.numpy as jnp
from jax import lax
from jax.experimental import pallas as pl
from jax.experimental.pallas import tpu as pltpu
from jax.sharding import PartitionSpec as P

AXES = ("dp", "fsdp")
F32, BF16 = jnp.float32, jnp.bfloat16
MIB = 1 << 20
VMEM = pl.BlockSpec(memory_space=pltpu.VMEM)
SMEM = pl.BlockSpec(memory_space=pltpu.SMEM)
ANY = pl.BlockSpec(memory_space=pl.ANY)


def shape(dims, dtype):
    return jax.ShapeDtypeStruct(dims, dtype)


def params(mib):
    return pltpu.CompilerParams(vmem_limit_bytes=mib * MIB)


def cost(flops, nbytes):
    return pl.CostEstimate(flops=int(flops), bytes_accessed=int(nbytes), transcendentals=0)


def place():
    d = lax.axis_index("dp")
    return d // 4, (d // 2) % 2, d % 2, lax.axis_index("fsdp")


def power(base, count):
    result, factor = F32(1.0), base
    for bit in range(31):
        result = jnp.where((count // (1 << bit)) % 2 == 1, result * F32(factor), result)
        factor = factor * factor
    return result


def plain(attn, cotangent, weight, projector, moment_one, moment_two, step_count):
    shard_rows = weight.shape[0]
    reduced = jnp.dot(attn, projector, preferred_element_type=F32).astype(BF16)
    grad_input = lax.dot_general(
        cotangent,
        lax.all_gather(weight, "fsdp", axis=0, tiled=True),
        (((1,), (1,)), ((), ())),
        preferred_element_type=F32,
    ).astype(BF16)
    projected = lax.psum_scatter(
        lax.dot_general(cotangent, reduced, (((0,), (0,)), ((), ())), preferred_element_type=F32),
        AXES,
        scatter_dimension=0,
        tiled=True,
    )
    first_moment = 0.9 * moment_one + 0.1 * projected
    second_moment = 0.999 * moment_two + 0.001 * projected * projected
    steps = step_count[0].astype(F32)
    first_hat = first_moment / (1.0 - jnp.power(F32(0.9), steps))
    second_hat = second_moment / (1.0 - jnp.power(F32(0.999), steps))
    low_step = (first_hat / (jnp.sqrt(second_hat) + 1e-08)).astype(BF16)
    my_projector = lax.dynamic_slice_in_dim(
        projector, lax.axis_index("fsdp") * shard_rows, shard_rows, 0
    )
    weight_step = 0.25 * lax.dot_general(
        my_projector,
        lax.all_gather(low_step, AXES, axis=0, tiled=True),
        (((1,), (1,)), ((), ())),
        preferred_element_type=F32,
    )
    return grad_input, weight_step, first_moment, second_moment


def solution(mesh):
    n_dp, n_y = mesh.shape["dp"], mesh.shape["fsdp"]
    n_z = n_dp // 4
    groups = 2 * n_z
    plane = [(dx, dy) for dx in range(2) for dy in range(n_y) if (dx, dy) != (0, 0)]

    def send(value, move):
        pairs = []
        for z in range(n_z):
            for x in range(2):
                for c in range(2):
                    for y in range(n_y):
                        tz, tx, tc, ty = move(z, x, c, y)
                        pairs.append(
                            (((z * 2 + x) * 2 + c) * n_y + y, ((tz * 2 + tx) * 2 + tc) * n_y + ty)
                        )
        return lax.ppermute(value, AXES, pairs)

    def to_core(value):
        return send(value, lambda z, x, c, y: (z, x, 1 - c, y))

    def to_plane(value, dx, dy):
        return send(value, lambda z, x, c, y: (z, x ^ dx, c, (y + dy) % n_y))

    def to_z(value, dz):
        return send(value, lambda z, x, c, y: ((z + dz) % n_z, x, c, y))

    def to_z_pair(value):
        return send(value, lambda z, x, c, y: (z ^ 1, x, c, y))

    def local_sums(attn, projector, cotangent):
        tokens, inner = attn.shape
        width, rank = cotangent.shape[1], projector.shape[1]
        rows = width // groups
        own = rows // (2 * n_y)

        def kernel(a_hbm, p_hbm, g_hbm, send_ref, keep_ref, a, p, g, red, part, sems):
            c = lax.axis_index("dp") % 2
            copy_a = pltpu.make_async_copy(a_hbm, a, sems.at[0])
            copy_p = pltpu.make_async_copy(p_hbm, p, sems.at[1])
            copy_a.start()
            copy_p.start()
            copies = []
            for k in range(groups):
                span = pl.ds(k * rows, rows)
                copies.append(pltpu.make_async_copy(g_hbm.at[:, span], g.at[k], sems.at[2 + k]))
                copies[-1].start()
            copy_a.wait()
            copy_p.wait()
            red[...] = jnp.dot(a[...], p[...], preferred_element_type=F32).astype(BF16)
            for k in range(groups):
                copies[k].wait()
                part[k % 2] = lax.dot_general(
                    g[k], red[...], (((0,), (0,)), ((), ())), preferred_element_type=F32
                )
                for y in range(n_y):
                    mine = pl.multiple_of(c * (n_y * own) + y * own, own)
                    theirs = pl.multiple_of((1 - c) * (n_y * own) + y * own, own)
                    keep_ref[k % 2, y, k // 2] = part[k % 2, pl.ds(mine, own), :]
                    send_ref[k % 2, y, k // 2] = part[k % 2, pl.ds(theirs, own), :].astype(BF16)

        dims = (2, n_y, n_z, own, rank)
        return pl.pallas_call(
            kernel,
            out_shape=(shape(dims, BF16), shape(dims, F32)),
            in_specs=[ANY, ANY, ANY],
            out_specs=(VMEM, VMEM),
            scratch_shapes=[
                pltpu.VMEM(attn.shape, BF16),
                pltpu.VMEM(projector.shape, BF16),
                pltpu.VMEM((groups, tokens, rows), BF16),
                pltpu.VMEM((tokens, rank), BF16),
                pltpu.VMEM((2, rows, rank), F32),
                pltpu.SemaphoreType.DMA((2 + groups,)),
            ],
            compiler_params=params(24),
            cost_estimate=cost(
                2 * tokens * rank * (inner + width), 2 * tokens * (inner + width) + 6 * width * rank
            ),
        )(attn, projector, cotangent)

    def core_sum(keep, got):
        slab = keep.shape[2:]

        def kernel(keep_ref, got_ref, own_ref, *send_refs):
            z, x, c, y = place()
            own_ref[...] = keep_ref[x, y] + got_ref[x, y].astype(F32)
            for (dx, dy), ref in zip(plane, send_refs):
                tx, ty = (x + dx) % 2, (y + dy) % n_y
                ref[...] = (keep_ref[tx, ty] + got_ref[tx, ty].astype(F32)).astype(BF16)

        return pl.pallas_call(
            kernel,
            out_shape=(shape(slab, F32),) + (shape(slab, BF16),) * len(plane),
            in_specs=[VMEM, VMEM],
            out_specs=(VMEM,) * (1 + len(plane)),
            compiler_params=params(12),
            cost_estimate=cost(keep.size, 8 * keep.size),
        )(keep, got)

    def plane_sum(own, got):
        slab = own.shape[1:]

        def kernel(own_ref, *refs):
            got_refs, out_ref, send_refs = refs[: len(got)], refs[len(got)], refs[len(got) + 1 :]
            z, x, c, y = place()
            for dz in range(n_z):
                tz = (z + dz) % n_z
                total = own_ref[tz]
                for ref in got_refs:
                    total = total + ref[tz].astype(F32)
                if dz == 0:
                    out_ref[...] = total
                else:
                    send_refs[dz - 1][...] = total.astype(BF16)

        return pl.pallas_call(
            kernel,
            out_shape=(shape(slab, F32),) + (shape(slab, BF16),) * (n_z - 1),
            in_specs=[VMEM] * (1 + len(got)),
            out_specs=(VMEM,) * n_z,
            compiler_params=params(8),
            cost_estimate=cost(4 * own.size, 10 * own.size),
        )(own, *got)

    def adam(own, got, moment_one, moment_two, step_count):
        def kernel(step_ref, own_ref, *refs):
            got_refs, (m1, m2, first_ref, second_ref, low_ref) = refs[: len(got)], refs[len(got) :]
            projected = own_ref[...]
            for ref in got_refs:
                projected = projected + ref[...].astype(F32)
            first = 0.9 * m1[...] + 0.1 * projected
            second = 0.999 * m2[...] + 0.001 * projected * projected
            first_ref[...] = first
            second_ref[...] = second
            count = step_ref[0]
            ones = jnp.ones(first.shape, F32)
            first_hat = first / ((1.0 - power(0.9, count)) * ones)
            second_hat = second / ((1.0 - power(0.999, count)) * ones)
            low_ref[...] = (first_hat / (jnp.sqrt(second_hat) + 1e-08)).astype(BF16)

        dims = own.shape
        return pl.pallas_call(
            kernel,
            out_shape=(shape(dims, F32), shape(dims, F32), shape(dims, BF16)),
            in_specs=[SMEM] + [VMEM] * (3 + len(got)),
            out_specs=(VMEM, VMEM, VMEM),
            compiler_params=params(4),
            cost_estimate=cost(20 * own.size, 24 * own.size),
        )(step_count, own, *got, moment_one, moment_two)

    def step_product(my_projector, blocks):
        rows, rank = my_projector.shape
        own = blocks[0][3].shape[1]
        span = 2 * n_y * own
        width = groups * span

        def kernel(p_ref, *refs):
            columns, (out_hbm, low, out, sems) = refs[: len(blocks)], refs[len(blocks) :]
            z, x, c, y = place()
            for (dc, dx, dy, _), ref in zip(blocks, columns):
                tc, tx, ty = (c + dc) % 2, (x + dx) % 2, (y + n_y - dy) % n_y
                for dz in range(n_z):
                    tz = (z + n_z - dz) % n_z
                    row = pl.multiple_of((tc * n_y + ty) * own, own)
                    low[tz * 2 + tx, pl.ds(row, own), :] = ref[dz]
            copies = []
            for k in range(groups):
                out[k] = 0.25 * lax.dot_general(
                    p_ref[...], low[k], (((1,), (1,)), ((), ())), preferred_element_type=F32
                )
                copies.append(
                    pltpu.make_async_copy(out.at[k], out_hbm.at[:, pl.ds(k * span, span)], sems.at[k])
                )
                copies[-1].start()
            for copy in copies:
                copy.wait()

        return pl.pallas_call(
            kernel,
            out_shape=shape((rows, width), F32),
            in_specs=[VMEM] * (1 + len(blocks)),
            out_specs=ANY,
            scratch_shapes=[
                pltpu.VMEM((groups, span, rank), BF16),
                pltpu.VMEM((groups, rows, span), F32),
                pltpu.SemaphoreType.DMA((groups,)),
            ],
            compiler_params=params(24),
            cost_estimate=cost(2 * rows * rank * width, 4 * rows * width),
        )(my_projector, *[block[3] for block in blocks])

    def input_product(cotangent, pieces, dy, into=None):
        tokens, width = cotangent.shape
        rows = sum(piece.shape[0] for _, piece in pieces)
        step = 256 if rows % 256 == 0 else 128
        chunks = rows // step

        def kernel(*refs):
            g_hbm, w_hbm = refs[0], refs[1 : 1 + len(pieces)]
            out_hbm, g, w, out, sems = refs[-5:]
            z, x, c, y = place()
            copy_g = pltpu.make_async_copy(g_hbm, g, sems.at[0])
            copy_g.start()
            copies = []
            for k, ((position, piece), ref) in enumerate(zip(pieces, w_hbm)):
                count = piece.shape[0]
                row = pl.multiple_of(position(z, x, c) * count, count)
                copies.append(pltpu.make_async_copy(ref, w.at[pl.ds(row, count)], sems.at[1 + k]))
                copies[-1].start()
            copy_g.wait()
            for copy in copies:
                copy.wait()
            outs = []
            base = ((y + n_y - dy) % n_y) * rows
            for k in range(chunks):
                out[k] = lax.dot_general(
                    g[...],
                    w[pl.ds(k * step, step), :],
                    (((1,), (1,)), ((), ())),
                    preferred_element_type=F32,
                ).astype(BF16)
                column = pl.multiple_of(base + k * step, step)
                outs.append(
                    pltpu.make_async_copy(
                        out.at[k], out_hbm.at[:, pl.ds(column, step)], sems.at[1 + len(pieces) + k]
                    )
                )
                outs[-1].start()
            for copy in outs:
                copy.wait()

        operands = [cotangent] + [piece for _, piece in pieces]
        aliases = {}
        if into is not None:
            operands.append(into)
            aliases = {len(operands) - 1: 0}
        return pl.pallas_call(
            kernel,
            out_shape=shape((tokens, rows * n_y), BF16),
            in_specs=[ANY] * len(operands),
            out_specs=ANY,
            input_output_aliases=aliases,
            scratch_shapes=[
                pltpu.VMEM(cotangent.shape, BF16),
                pltpu.VMEM((rows, width), BF16),
                pltpu.VMEM((chunks, tokens, step), BF16),
                pltpu.SemaphoreType.DMA((1 + len(pieces) + chunks,)),
            ],
            compiler_params=params(24),
            cost_estimate=cost(2 * tokens * rows * width, 2 * (tokens + rows) * width),
        )(*operands)

    def on_device(attn, cotangent, weight, projector, moment_one, moment_two, step_count):
        shard_rows, width = weight.shape
        own_rows = moment_one.shape[0]
        if n_y != 2 or own_rows % 16 or shard_rows % 128 or n_z % 2:
            return plain(attn, cotangent, weight, projector, moment_one, moment_two, step_count)
        z, x, c, y = place()
        q = (x * 2 + z % 2) * 2 + c

        own = to_plane(
            lax.dynamic_slice_in_dim(weight, q * (shard_rows // 8), shard_rows // 8, 0), 0, 1
        )
        over_x = to_plane(own, 1, 0)
        over_z = to_z_pair(own)
        over_xz = to_z_pair(over_x)
        pieces = []
        for dx, dz, piece in ((0, 0, own), (1, 0, over_x), (0, 1, over_z), (1, 1, over_xz)):
            for dc in range(2):
                position = lambda z, x, c, dx=dx, dz=dz, dc=dc: (
                    ((x + dx) % 2) * 2 + (z + dz) % 2
                ) * 2 + (c + dc) % 2
                pieces.append((position, to_core(piece) if dc else piece))

        outgoing, keep = local_sums(attn, projector, cotangent)
        sums = core_sum(keep, to_core(outgoing))
        got = [to_plane(part, dx, dy) for (dx, dy), part in zip(plane, sums[1:])]
        sums = plane_sum(sums[0], got)
        got = [to_z(part, dz) for dz, part in zip(range(1, n_z), sums[1:])]
        first_moment, second_moment, low_step = adam(
            sums[0], got, moment_one, moment_two, step_count
        )
        column = jnp.stack([low_step] + [to_z(low_step, dz) for dz in range(1, n_z)])
        blocks = [(0, 0, 0, column), (1, 0, 0, to_core(column))]
        for dx, dy in plane:
            got = to_plane(column, dx, dy)
            blocks += [(0, dx, dy, got), (1, dx, dy, to_core(got))]
        my_projector = lax.dynamic_slice_in_dim(projector, y * shard_rows, shard_rows, 0)
        weight_step = step_product(my_projector, blocks)

        grad_input = input_product(cotangent, [(lambda z, x, c: 0, weight)], 0)
        grad_input = input_product(cotangent, pieces, 1, grad_input)
        return grad_input, weight_step, first_moment, second_moment

    rows = P(("dp", "fsdp"), None)
    return jax.shard_map(
        on_device,
        mesh=mesh,
        in_specs=(rows, rows, P("fsdp", None), P(), rows, rows, P()),
        out_specs=(rows, P("fsdp", None), rows, rows),
        check_vma=False,
    )
```

```python
import jax
import jax.numpy as jnp
from jax import lax
from jax.experimental import pallas as pl
from jax.experimental.pallas import tpu as pltpu
from jax.sharding import PartitionSpec as P

AXES = ("dp", "fsdp")
F32, BF16 = jnp.float32, jnp.bfloat16
MIB = 1 << 20
VMEM = pl.BlockSpec(memory_space=pltpu.VMEM)
SMEM = pl.BlockSpec(memory_space=pltpu.SMEM)
ANY = pl.BlockSpec(memory_space=pl.ANY)
HBM = pl.BlockSpec(memory_space=pltpu.HBM)


def shape(dims, dtype):
    return jax.ShapeDtypeStruct(dims, dtype)


def params(mib):
    return pltpu.CompilerParams(vmem_limit_bytes=int(mib * MIB))


def cost(flops, nbytes):
    return pl.CostEstimate(flops=0, bytes_accessed=0, transcendentals=0)


def place():
    d = lax.axis_index("dp")
    return d // 4, (d // 2) % 2, d % 2, lax.axis_index("fsdp")


def power(base, count):
    result, factor = F32(1.0), base
    for bit in range(31):
        result = jnp.where((count // (1 << bit)) % 2 == 1, result * F32(factor), result)
        factor = factor * factor
    return result


def plain(attn, cotangent, weight, projector, moment_one, moment_two, step_count):
    shard_rows = weight.shape[0]
    reduced = jnp.dot(attn, projector, preferred_element_type=F32).astype(BF16)
    grad_input = lax.dot_general(
        cotangent,
        lax.all_gather(weight, "fsdp", axis=0, tiled=True),
        (((1,), (1,)), ((), ())),
        preferred_element_type=F32,
    ).astype(BF16)
    projected = lax.psum_scatter(
        lax.dot_general(cotangent, reduced, (((0,), (0,)), ((), ())), preferred_element_type=F32),
        AXES,
        scatter_dimension=0,
        tiled=True,
    )
    first_moment = 0.9 * moment_one + 0.1 * projected
    second_moment = 0.999 * moment_two + 0.001 * projected * projected
    steps = step_count[0].astype(F32)
    first_hat = first_moment / (1.0 - jnp.power(F32(0.9), steps))
    second_hat = second_moment / (1.0 - jnp.power(F32(0.999), steps))
    low_step = (first_hat / (jnp.sqrt(second_hat) + 1e-08)).astype(BF16)
    my_projector = lax.dynamic_slice_in_dim(
        projector, lax.axis_index("fsdp") * shard_rows, shard_rows, 0
    )
    weight_step = 0.25 * lax.dot_general(
        my_projector,
        lax.all_gather(low_step, AXES, axis=0, tiled=True),
        (((1,), (1,)), ((), ())),
        preferred_element_type=F32,
    )
    return grad_input, weight_step, first_moment, second_moment


def solution(mesh):
    n_dp, n_y = mesh.shape["dp"], mesh.shape["fsdp"]
    n_z = n_dp // 4
    groups = 2 * n_z
    plane = [(dx, dy) for dx in range(2) for dy in range(n_y) if (dx, dy) != (0, 0)]

    def send(value, move):
        pairs = []
        for z in range(n_z):
            for x in range(2):
                for c in range(2):
                    for y in range(n_y):
                        tz, tx, tc, ty = move(z, x, c, y)
                        pairs.append(
                            (((z * 2 + x) * 2 + c) * n_y + y, ((tz * 2 + tx) * 2 + tc) * n_y + ty)
                        )
        return lax.ppermute(value, AXES, pairs)

    def to_core(value):
        return send(value, lambda z, x, c, y: (z, x, 1 - c, y))

    def to_plane(value, dx, dy):
        return send(value, lambda z, x, c, y: (z, x ^ dx, c, (y + dy) % n_y))

    def to_z(value, dz):
        return send(value, lambda z, x, c, y: ((z + dz) % n_z, x, c, y))

    def to_z_pair(value):
        return send(value, lambda z, x, c, y: (z ^ 1, x, c, y))

    def local_sums(attn, projector, cotangent):
        tokens, inner = attn.shape
        width, rank = cotangent.shape[1], projector.shape[1]
        rows = width // groups
        own = rows // (2 * n_y)

        def kernel(a_hbm, p_hbm, g_hbm, send_ref, keep_ref, a, p, g, red, part, sems):
            c = lax.axis_index("dp") % 2
            copy_a = pltpu.make_async_copy(a_hbm, a, sems.at[0])
            copy_p = pltpu.make_async_copy(p_hbm, p, sems.at[1])
            copy_a.start()
            copy_p.start()
            copies = []
            for k in range(groups):
                span = pl.ds(k * rows, rows)
                copies.append(pltpu.make_async_copy(g_hbm.at[:, span], g.at[k], sems.at[2 + k]))
                copies[-1].start()
            copy_a.wait()
            copy_p.wait()
            red[...] = jnp.dot(a[...], p[...], preferred_element_type=F32).astype(BF16)
            for k in range(groups):
                copies[k].wait()
                part[k % 2] = lax.dot_general(
                    g[k], red[...], (((0,), (0,)), ((), ())), preferred_element_type=F32
                )
                for y in range(n_y):
                    mine = pl.multiple_of(c * (n_y * own) + y * own, own)
                    theirs = pl.multiple_of((1 - c) * (n_y * own) + y * own, own)
                    keep_ref[k % 2, y, k // 2] = part[k % 2, pl.ds(mine, own), :]
                    send_ref[k % 2, y, k // 2] = part[k % 2, pl.ds(theirs, own), :].astype(BF16)

        dims = (2, n_y, n_z, own, rank)
        return pl.pallas_call(
            kernel,
            out_shape=(shape(dims, BF16), shape(dims, F32)),
            in_specs=[HBM, HBM, HBM],
            out_specs=(VMEM, VMEM),
            scratch_shapes=[
                pltpu.VMEM(attn.shape, BF16),
                pltpu.VMEM(projector.shape, BF16),
                pltpu.VMEM((groups, tokens, rows), BF16),
                pltpu.VMEM((tokens, rank), BF16),
                pltpu.VMEM((2, rows, rank), F32),
                pltpu.SemaphoreType.DMA((2 + groups,)),
            ],
            compiler_params=params(50),
            cost_estimate=cost(
                2 * tokens * rank * (inner + width), 2 * tokens * (inner + width) + 6 * width * rank
            ),
        )(attn, projector, cotangent)

    def core_sum(keep, got):
        slab = keep.shape[2:]

        def kernel(keep_ref, got_ref, own_ref, *send_refs):
            z, x, c, y = place()
            own_ref[...] = keep_ref[x, y] + got_ref[x, y].astype(F32)
            for (dx, dy), ref in zip(plane, send_refs):
                tx, ty = (x + dx) % 2, (y + dy) % n_y
                ref[...] = (keep_ref[tx, ty] + got_ref[tx, ty].astype(F32)).astype(BF16)

        return pl.pallas_call(
            kernel,
            out_shape=(shape(slab, F32),) + (shape(slab, BF16),) * len(plane),
            in_specs=[VMEM, VMEM],
            out_specs=(VMEM,) * (1 + len(plane)),
            compiler_params=params(12),
            cost_estimate=cost(keep.size, 8 * keep.size),
        )(keep, got)

    def plane_sum(own, got, parts, wait):
        slab = own.shape[1:]
        rows, width = sum(part.shape[0] for part in parts), parts[0].shape[1]

        def kernel(own_ref, *refs):
            got_refs, part_refs = refs[: len(got)], refs[len(got) : len(got) + len(parts)]
            out_ref, send_refs = refs[-2 - n_z], refs[-1 - n_z : -2]
            full_ref, half_ref = refs[-2:]
            z, x, c, y = place()
            for dz in range(n_z):
                tz = (z + dz) % n_z
                total = own_ref[tz]
                for ref in got_refs:
                    total = total + ref[tz].astype(F32)
                if dz == 0:
                    out_ref[...] = total
                else:
                    send_refs[dz - 1][...] = total.astype(BF16)
            begin = 0
            for ref in part_refs:
                full_ref[begin : begin + ref.shape[0], :] = ref[...]
                begin += ref.shape[0]
            half_ref[...] = full_ref[: rows // 2, :]

        return pl.pallas_call(
            kernel,
            out_shape=(shape(slab, F32),)
            + (shape(slab, BF16),) * (n_z - 1)
            + (shape((rows, width), BF16), shape((rows // 2, width), BF16)),
            in_specs=[VMEM] * (1 + len(got) + len(parts)) + [ANY] * len(wait),
            out_specs=(VMEM,) * (n_z + 2),
            compiler_params=params(8),
            cost_estimate=cost(4 * own.size, 10 * own.size),
        )(own, *got, *parts, *wait)

    def adam(own, got, moment_one, moment_two, step_count, full, wait):
        half = full.shape[0] // 2

        def kernel(step_ref, own_ref, *refs):
            got_refs, (m1, m2, full_ref, wait_ref) = refs[: len(got)], refs[len(got) : -4]
            first_ref, second_ref, low_ref, half_ref = refs[-4:]
            half_ref[...] = full_ref[half:, :]
            projected = own_ref[...]
            for ref in got_refs:
                projected = projected + ref[...].astype(F32)
            first = 0.9 * m1[...] + 0.1 * projected
            second = 0.999 * m2[...] + 0.001 * projected * projected
            first_ref[...] = first
            second_ref[...] = second
            count = step_ref[0]
            ones = jnp.ones(first.shape, F32)
            first_hat = first / ((1.0 - power(0.9, count)) * ones)
            second_hat = second / ((1.0 - power(0.999, count)) * ones)
            low_ref[...] = (first_hat / (jnp.sqrt(second_hat) + 1e-08)).astype(BF16)

        dims = own.shape
        return pl.pallas_call(
            kernel,
            out_shape=(
                shape(dims, F32),
                shape(dims, F32),
                shape(dims, BF16),
                shape((half, full.shape[1]), BF16),
            ),
            in_specs=[SMEM] + [VMEM] * (4 + len(got)) + [ANY],
            out_specs=(VMEM,) * 4,
            compiler_params=params(4),
            cost_estimate=cost(20 * own.size, 24 * own.size),
        )(step_count, own, *got, moment_one, moment_two, full, wait)

    def step_product(my_projector, blocks):
        rows, rank = my_projector.shape
        own = blocks[0][3].shape[1]
        span = 2 * n_y * own
        width = groups * span

        def kernel(p_ref, *refs):
            columns, (out_hbm, low, out, sems) = refs[: len(blocks)], refs[len(blocks) :]
            z, x, c, y = place()
            for (dc, dx, dy, _), ref in zip(blocks, columns):
                tc, tx, ty = (c + dc) % 2, (x + dx) % 2, (y + n_y - dy) % n_y
                for dz in range(n_z):
                    tz = (z + n_z - dz) % n_z
                    row = pl.multiple_of((tc * n_y + ty) * own, own)
                    low[tz * 2 + tx, pl.ds(row, own), :] = ref[dz]
            copies = []
            for k in range(groups):
                out[k] = 0.25 * lax.dot_general(
                    p_ref[...], low[k], (((1,), (1,)), ((), ())), preferred_element_type=F32
                )
                copies.append(
                    pltpu.make_async_copy(out.at[k], out_hbm.at[:, pl.ds(k * span, span)], sems.at[k])
                )
                copies[-1].start()
            for copy in copies:
                copy.wait()

        return pl.pallas_call(
            kernel,
            out_shape=shape((rows, width), F32),
            in_specs=[VMEM] * (1 + len(blocks)),
            out_specs=HBM,
            scratch_shapes=[
                pltpu.VMEM((groups, span, rank), BF16),
                pltpu.VMEM((groups, rows, span), F32),
                pltpu.SemaphoreType.DMA((groups,)),
            ],
            compiler_params=params(16),
            cost_estimate=cost(2 * rows * rank * width, 4 * rows * width),
        )(my_projector, *[block[3] for block in blocks])

    def own_product(cotangent, weight, wait):
        tokens, width = cotangent.shape
        rows = weight.shape[0]
        step = 256
        chunks = rows // step

        def kernel(g_hbm, w_hbm, wait_ref, out_hbm, done_ref, g, w, out, sems):
            y = lax.axis_index("fsdp")
            copy_g = pltpu.make_async_copy(g_hbm, g, sems.at[0])
            copy_g.start()
            copies = []
            for k in range(chunks):
                copies.append(
                    pltpu.make_async_copy(
                        w_hbm.at[pl.ds(k * step, step), :], w.at[k], sems.at[1 + k]
                    )
                )
                copies[-1].start()
            done_ref[...] = jnp.zeros_like(done_ref)
            copy_g.wait()
            outs = []
            for k in range(chunks):
                copies[k].wait()
                out[k] = lax.dot_general(
                    g[...], w[k], (((1,), (1,)), ((), ())), preferred_element_type=F32
                ).astype(BF16)
                column = pl.multiple_of(y * rows + k * step, step)
                outs.append(
                    pltpu.make_async_copy(
                        out.at[k], out_hbm.at[:, pl.ds(column, step)], sems.at[1 + chunks + k]
                    )
                )
                outs[-1].start()
            for copy in outs:
                copy.wait()

        return pl.pallas_call(
            kernel,
            out_shape=(shape((tokens, rows * n_y), BF16), shape((8, 128), F32)),
            in_specs=[HBM, HBM, ANY],
            out_specs=(HBM, VMEM),
            scratch_shapes=[
                pltpu.VMEM((tokens, width), BF16),
                pltpu.VMEM((chunks, step, width), BF16),
                pltpu.VMEM((chunks, tokens, step), BF16),
                pltpu.SemaphoreType.DMA((1 + 2 * chunks,)),
            ],
            compiler_params=params(50),
            cost_estimate=cost(2 * tokens * rows * width, 2 * (tokens + rows) * width),
        )(cotangent, weight, wait)

    def stack(values, *wait):
        def kernel(*refs):
            for k in range(len(values)):
                refs[-1][k] = refs[k][...]

        return pl.pallas_call(
            kernel,
            out_shape=shape((len(values),) + values[0].shape, values[0].dtype),
            in_specs=[VMEM] * len(values) + [ANY] * len(wait),
            out_specs=VMEM,
            compiler_params=params(4),
            cost_estimate=cost(0, 2 * values[0].size),
        )(*values, *wait)

    def relay(value, *wait):
        def kernel(ref, *refs):
            refs[-1][...] = ref[...]

        return pl.pallas_call(
            kernel,
            out_shape=shape(value.shape, value.dtype),
            in_specs=[VMEM] + [ANY] * len(wait),
            out_specs=VMEM,
            compiler_params=params(4),
            cost_estimate=cost(0, 2 * value.size),
        )(value, *wait)

    def other_product(cotangent, pieces, into):
        tokens, width = cotangent.shape
        rows = sum(piece.shape[0] for _, piece in pieces)
        step = 256 if rows % 256 == 0 else 128
        chunks = rows // step

        def kernel(g_ref, *refs):
            w_refs = refs[: len(pieces)]
            out_hbm, w, out, sems = refs[-4:]
            z, x, c, y = place()
            copies = []
            for k, ((first, piece), ref) in enumerate(zip(pieces, w_refs)):
                count = piece.shape[0]
                row = pl.multiple_of(first(z, x, c), 16)
                copies.append(pltpu.make_async_copy(ref, w.at[pl.ds(row, count)], sems.at[k]))
                copies[-1].start()
            for copy in copies:
                copy.wait()
            outs = []
            for k in range(chunks):
                out[k] = lax.dot_general(
                    g_ref[...],
                    w[pl.ds(k * step, step), :],
                    (((1,), (1,)), ((), ())),
                    preferred_element_type=F32,
                ).astype(BF16)
                column = pl.multiple_of((1 - y) * rows + k * step, step)
                outs.append(
                    pltpu.make_async_copy(
                        out.at[k], out_hbm.at[:, pl.ds(column, step)], sems.at[len(pieces) + k]
                    )
                )
                outs[-1].start()
            for copy in outs:
                copy.wait()

        return pl.pallas_call(
            kernel,
            out_shape=shape(into.shape, BF16),
            in_specs=[VMEM] + [ANY] * len(pieces) + [HBM],
            out_specs=HBM,
            input_output_aliases={1 + len(pieces): 0},
            scratch_shapes=[
                pltpu.VMEM((rows, width), BF16),
                pltpu.VMEM((chunks, tokens, step), BF16),
                pltpu.SemaphoreType.DMA((len(pieces) + chunks,)),
            ],
            compiler_params=params(8),
            cost_estimate=cost(2 * tokens * rows * width, 2 * (tokens + rows) * width),
        )(cotangent, *[piece for _, piece in pieces], into)

    def on_device(attn, cotangent, weight, projector, moment_one, moment_two, step_count):
        shard_rows, width = weight.shape
        own_rows = moment_one.shape[0]
        if n_y != 2 or own_rows % 16 or shard_rows % 384 or n_z % 2:
            return plain(attn, cotangent, weight, projector, moment_one, moment_two, step_count)
        z, x, c, y = place()
        q = (x * 2 + z % 2) * 2 + c

        eighth = shard_rows // 8
        cut = eighth // 48 * 16
        cuts = ((0, cut), (cut, eighth - cut))

        def mine(part):
            begin, count = cuts[part]
            return lax.dynamic_slice_in_dim(weight, q * eighth + begin, count, 0)

        outgoing, keep = local_sums(attn, projector, cotangent)
        over_y = [to_plane(mine(0), 0, 1)]
        over_y.append(to_plane(relay(mine(1), over_y[0]), 0, 1))
        sums = core_sum(keep, to_core(relay(outgoing, over_y[0])))
        over_z = [to_z_pair(over_y[0])]

        got = [to_plane(part, dx, dy) for (dx, dy), part in zip(plane, sums[1:])]
        grad_input, done = own_product(cotangent, weight, sums[1])
        over_y[1] = relay(over_y[1], done)
        over_z.append(to_z_pair(over_y[1]))
        sums = plane_sum(sums[0], got, over_y, [over_z[0]])
        own, half = sums[n_z:]

        over_x = [to_plane(half, 1, 0)]
        got = [to_z(part, dz) for dz, part in zip(range(1, n_z), sums[1:n_z])]
        first_moment, second_moment, low_step, half = adam(
            sums[0], got, moment_one, moment_two, step_count, own, over_x[0]
        )
        over_x.append(to_plane(half, 1, 0))
        over_xz = [to_z_pair(part) for part in over_x]
        column = stack(
            [low_step] + [to_z(low_step, dz) for dz in range(1, n_z)], over_z[1], over_x[1]
        )

        blocks = [(0, 0, 0, column), (1, 0, 0, to_core(column))]
        for dx, dy in plane:
            got = to_plane(column, dx, dy)
            blocks += [(0, dx, dy, got), (1, dx, dy, to_core(got))]
        pieces = []
        for dx, dz, parts in ((0, 0, [own]), (1, 0, over_x), (0, 1, over_z), (1, 1, over_xz)):
            begin = 0
            for part in parts:
                for dc in range(2):
                    row = lambda z, x, c, dx=dx, dz=dz, dc=dc, begin=begin: (
                        (((x + dx) % 2) * 2 + (z + dz) % 2) * 2 + (c + dc) % 2
                    ) * eighth + begin
                    pieces.append((row, to_core(part) if dc else part))
                begin += part.shape[0]
        my_projector = lax.dynamic_slice_in_dim(projector, y * shard_rows, shard_rows, 0)
        weight_step = step_product(my_projector, blocks)

        grad_input = other_product(cotangent, pieces, grad_input)
        return grad_input, weight_step, first_moment, second_moment

    rows = P(("dp", "fsdp"), None)
    return jax.shard_map(
        on_device,
        mesh=mesh,
        in_specs=(rows, rows, P("fsdp", None), P(), rows, rows, P()),
        out_specs=(rows, P("fsdp", None), rows, rows),
        check_vma=False,
    )
```

```python
import jax
import jax.numpy as jnp
from jax import lax
from jax.experimental import pallas as pl
from jax.experimental.pallas import tpu as pltpu
from jax.sharding import PartitionSpec as P

AXES = ("dp", "fsdp")
F32, BF16 = jnp.float32, jnp.bfloat16
MIB = 1 << 20
VMEM = pl.BlockSpec(memory_space=pltpu.VMEM)
SMEM = pl.BlockSpec(memory_space=pltpu.SMEM)
ANY = pl.BlockSpec(memory_space=pl.ANY)
HBM = pl.BlockSpec(memory_space=pltpu.HBM)


def shape(dims, dtype):
    return jax.ShapeDtypeStruct(dims, dtype)


def params(mib):
    return pltpu.CompilerParams(vmem_limit_bytes=int(mib * MIB))


def cost(flops, nbytes):
    return pl.CostEstimate(flops=0, bytes_accessed=0, transcendentals=0)


def place():
    d = lax.axis_index("dp")
    return d // 4, (d // 2) % 2, d % 2, lax.axis_index("fsdp")


def power(base, count):
    result, factor = F32(1.0), base
    for bit in range(31):
        result = jnp.where((count // (1 << bit)) % 2 == 1, result * F32(factor), result)
        factor = factor * factor
    return result


def plain(attn, cotangent, weight, projector, moment_one, moment_two, step_count):
    shard_rows = weight.shape[0]
    reduced = jnp.dot(attn, projector, preferred_element_type=F32).astype(BF16)
    grad_input = lax.dot_general(
        cotangent,
        lax.all_gather(weight, "fsdp", axis=0, tiled=True),
        (((1,), (1,)), ((), ())),
        preferred_element_type=F32,
    ).astype(BF16)
    projected = lax.psum_scatter(
        lax.dot_general(cotangent, reduced, (((0,), (0,)), ((), ())), preferred_element_type=F32),
        AXES,
        scatter_dimension=0,
        tiled=True,
    )
    first_moment = 0.9 * moment_one + 0.1 * projected
    second_moment = 0.999 * moment_two + 0.001 * projected * projected
    steps = step_count[0].astype(F32)
    first_hat = first_moment / (1.0 - jnp.power(F32(0.9), steps))
    second_hat = second_moment / (1.0 - jnp.power(F32(0.999), steps))
    low_step = (first_hat / (jnp.sqrt(second_hat) + 1e-08)).astype(BF16)
    my_projector = lax.dynamic_slice_in_dim(
        projector, lax.axis_index("fsdp") * shard_rows, shard_rows, 0
    )
    weight_step = 0.25 * lax.dot_general(
        my_projector,
        lax.all_gather(low_step, AXES, axis=0, tiled=True),
        (((1,), (1,)), ((), ())),
        preferred_element_type=F32,
    )
    return grad_input, weight_step, first_moment, second_moment


def solution(mesh):
    n_dp, n_y = mesh.shape["dp"], mesh.shape["fsdp"]
    n_z = n_dp // 4
    groups = 2 * n_z
    plane = [(dx, dy) for dx in range(2) for dy in range(n_y) if (dx, dy) != (0, 0)]

    def send(value, move):
        pairs = []
        for z in range(n_z):
            for x in range(2):
                for c in range(2):
                    for y in range(n_y):
                        tz, tx, tc, ty = move(z, x, c, y)
                        pairs.append(
                            (((z * 2 + x) * 2 + c) * n_y + y, ((tz * 2 + tx) * 2 + tc) * n_y + ty)
                        )
        return lax.ppermute(value, AXES, pairs)

    def to_core(value):
        return send(value, lambda z, x, c, y: (z, x, 1 - c, y))

    def to_plane(value, dx, dy):
        return send(value, lambda z, x, c, y: (z, x ^ dx, c, (y + dy) % n_y))

    def to_z(value, dz):
        return send(value, lambda z, x, c, y: ((z + dz) % n_z, x, c, y))

    def to_z_pair(value):
        return send(value, lambda z, x, c, y: (z ^ 1, x, c, y))

    def cut(weight, projector):
        rows, width = weight.shape
        eighth = rows // 8

        def kernel(w_hbm, p_hbm, first_ref, second_ref, p_ref, sems):
            z, x, c, y = place()
            row = pl.multiple_of(((x * 2 + z % 2) * 2 + c) * eighth, eighth)
            copies = [
                pltpu.make_async_copy(w_hbm.at[pl.ds(row, eighth // 2)], first_ref, sems.at[0]),
                pltpu.make_async_copy(
                    w_hbm.at[pl.ds(row + eighth // 2, eighth // 2)], second_ref, sems.at[1]
                ),
                pltpu.make_async_copy(p_hbm, p_ref, sems.at[2]),
            ]
            for copy in copies:
                copy.start()
            for copy in copies:
                copy.wait()

        half = shape((eighth // 2, width), BF16)
        return pl.pallas_call(
            kernel,
            out_shape=(half, half, shape(projector.shape, BF16)),
            in_specs=[HBM, HBM],
            out_specs=(VMEM,) * 3,
            scratch_shapes=[pltpu.SemaphoreType.DMA((3,))],
            compiler_params=params(54),
            cost_estimate=cost(0, 0),
        )(weight, projector)

    def local_sums(attn, projector, cotangent):
        tokens, inner = attn.shape
        width, rank = cotangent.shape[1], projector.shape[1]
        rows = width // groups
        own = rows // (2 * n_y)

        def kernel(a_hbm, p, g_hbm, send_ref, keep_ref, a, g, red, part, sems):
            c = lax.axis_index("dp") % 2
            copy_a = pltpu.make_async_copy(a_hbm, a, sems.at[0])
            copy_a.start()
            copies = []
            for k in range(groups):
                span = pl.ds(k * rows, rows)
                copies.append(pltpu.make_async_copy(g_hbm.at[:, span], g.at[k], sems.at[1 + k]))
                copies[-1].start()
            copy_a.wait()
            red[...] = jnp.dot(a[...], p[...], preferred_element_type=F32).astype(BF16)
            for k in range(groups):
                copies[k].wait()
                part[k % 2] = lax.dot_general(
                    g[k], red[...], (((0,), (0,)), ((), ())), preferred_element_type=F32
                )
                for y in range(n_y):
                    mine = pl.multiple_of(c * (n_y * own) + y * own, own)
                    theirs = pl.multiple_of((1 - c) * (n_y * own) + y * own, own)
                    keep_ref[k % 2, y, k // 2] = part[k % 2, pl.ds(mine, own), :]
                    send_ref[k % 2, y, k // 2] = part[k % 2, pl.ds(theirs, own), :].astype(BF16)

        dims = (2, n_y, n_z, own, rank)
        return pl.pallas_call(
            kernel,
            out_shape=(shape(dims, BF16), shape(dims, F32)),
            in_specs=[HBM, VMEM, HBM],
            out_specs=(VMEM, VMEM),
            scratch_shapes=[
                pltpu.VMEM(attn.shape, BF16),
                pltpu.VMEM((groups, tokens, rows), BF16),
                pltpu.VMEM((tokens, rank), BF16),
                pltpu.VMEM((2, rows, rank), F32),
                pltpu.SemaphoreType.DMA((1 + groups,)),
            ],
            compiler_params=params(50),
            cost_estimate=cost(
                2 * tokens * rank * (inner + width), 2 * tokens * (inner + width) + 6 * width * rank
            ),
        )(attn, projector, cotangent)

    def core_sum(keep, got):
        slab = keep.shape[2:]

        def kernel(keep_ref, got_ref, own_ref, *send_refs):
            z, x, c, y = place()
            own_ref[...] = keep_ref[x, y] + got_ref[x, y].astype(F32)
            for (dx, dy), ref in zip(plane, send_refs):
                tx, ty = (x + dx) % 2, (y + dy) % n_y
                ref[...] = (keep_ref[tx, ty] + got_ref[tx, ty].astype(F32)).astype(BF16)

        return pl.pallas_call(
            kernel,
            out_shape=(shape(slab, F32),) + (shape(slab, BF16),) * len(plane),
            in_specs=[VMEM, VMEM],
            out_specs=(VMEM,) * (1 + len(plane)),
            compiler_params=params(12),
            cost_estimate=cost(keep.size, 8 * keep.size),
        )(keep, got)

    def plane_sum(own, got, parts, wait):
        slab = own.shape[1:]
        rows, width = sum(part.shape[0] for part in parts), parts[0].shape[1]

        def kernel(own_ref, *refs):
            got_refs, part_refs = refs[: len(got)], refs[len(got) : len(got) + len(parts)]
            out_ref, send_refs, full_ref = refs[-1 - n_z], refs[-n_z:-1], refs[-1]
            z, x, c, y = place()
            for dz in range(n_z):
                tz = (z + dz) % n_z
                total = own_ref[tz]
                for ref in got_refs:
                    total = total + ref[tz].astype(F32)
                if dz == 0:
                    out_ref[...] = total
                else:
                    send_refs[dz - 1][...] = total.astype(BF16)
            begin = 0
            for ref in part_refs:
                full_ref[begin : begin + ref.shape[0], :] = ref[...]
                begin += ref.shape[0]

        return pl.pallas_call(
            kernel,
            out_shape=(shape(slab, F32),)
            + (shape(slab, BF16),) * (n_z - 1)
            + (shape((rows, width), BF16),),
            in_specs=[VMEM] * (1 + len(got) + len(parts)) + [ANY] * len(wait),
            out_specs=(VMEM,) * (n_z + 1),
            compiler_params=params(8),
            cost_estimate=cost(4 * own.size, 10 * own.size),
        )(own, *got, *parts, *wait)

    def adam(own, got, moment_one, moment_two, step_count):
        def kernel(step_ref, own_ref, *refs):
            got_refs, (m1, m2, first_ref, second_ref, low_ref) = refs[: len(got)], refs[len(got) :]
            projected = own_ref[...]
            for ref in got_refs:
                projected = projected + ref[...].astype(F32)
            first = 0.9 * m1[...] + 0.1 * projected
            second = 0.999 * m2[...] + 0.001 * projected * projected
            first_ref[...] = first
            second_ref[...] = second
            count = step_ref[0]
            ones = jnp.ones(first.shape, F32)
            first_hat = first / ((1.0 - power(0.9, count)) * ones)
            second_hat = second / ((1.0 - power(0.999, count)) * ones)
            low_ref[...] = (first_hat / (jnp.sqrt(second_hat) + 1e-08)).astype(BF16)

        dims = own.shape
        return pl.pallas_call(
            kernel,
            out_shape=(
                shape(dims, F32),
                shape(dims, F32),
                shape(dims, BF16),
            ),
            in_specs=[SMEM] + [VMEM] * (3 + len(got)),
            out_specs=(VMEM,) * 3,
            compiler_params=params(4),
            cost_estimate=cost(20 * own.size, 24 * own.size),
        )(step_count, own, *got, moment_one, moment_two)

    def step_product(projector, rows, blocks):
        rank = projector.shape[1]
        own = blocks[0][3].shape[1]
        span = 2 * n_y * own
        width = groups * span

        def kernel(p_ref, *refs):
            columns, (out_hbm, low, out, sems) = refs[: len(blocks)], refs[len(blocks) :]
            z, x, c, y = place()
            for (dc, dx, dy, _), ref in zip(blocks, columns):
                tc, tx, ty = (c + dc) % 2, (x + dx) % 2, (y + n_y - dy) % n_y
                for dz in range(n_z):
                    tz = (z + n_z - dz) % n_z
                    row = pl.multiple_of((tc * n_y + ty) * own, own)
                    low[tz * 2 + tx, pl.ds(row, own), :] = ref[dz]
            copies = []
            for k in range(groups):
                out[k] = 0.25 * lax.dot_general(
                    p_ref[pl.ds(pl.multiple_of(y * rows, 16), rows), :],
                    low[k],
                    (((1,), (1,)), ((), ())),
                    preferred_element_type=F32,
                )
                copies.append(
                    pltpu.make_async_copy(out.at[k], out_hbm.at[:, pl.ds(k * span, span)], sems.at[k])
                )
                copies[-1].start()
            for copy in copies:
                copy.wait()

        return pl.pallas_call(
            kernel,
            out_shape=shape((rows, width), F32),
            in_specs=[VMEM] * (1 + len(blocks)),
            out_specs=HBM,
            scratch_shapes=[
                pltpu.VMEM((groups, span, rank), BF16),
                pltpu.VMEM((groups, rows, span), F32),
                pltpu.SemaphoreType.DMA((groups,)),
            ],
            compiler_params=params(16),
            cost_estimate=cost(2 * rows * rank * width, 4 * rows * width),
        )(projector, *[block[3] for block in blocks])

    def own_product(cotangent, weight, *wait):
        tokens, width = cotangent.shape
        rows = weight.shape[0]
        step = 256
        chunks = rows // step

        def kernel(g, w_hbm, wait_ref, plane_ref, out_hbm, done_ref, w, out, sems):
            y = lax.axis_index("fsdp")
            copies = []
            for k in range(chunks):
                copies.append(
                    pltpu.make_async_copy(
                        w_hbm.at[pl.ds(k * step, step), :], w.at[k], sems.at[k]
                    )
                )
                copies[-1].start()
            done_ref[...] = jnp.zeros_like(done_ref)
            outs = []
            for k in range(chunks):
                copies[k].wait()
                out[k] = lax.dot_general(
                    g[...], w[k], (((1,), (1,)), ((), ())), preferred_element_type=F32
                ).astype(BF16)
                column = pl.multiple_of(y * rows + k * step, step)
                outs.append(
                    pltpu.make_async_copy(
                        out.at[k], out_hbm.at[:, pl.ds(column, step)], sems.at[chunks + k]
                    )
                )
                outs[-1].start()
            for copy in outs:
                copy.wait()

        return pl.pallas_call(
            kernel,
            out_shape=(shape((tokens, rows * n_y), BF16), shape((8, 128), F32)),
            in_specs=[VMEM, HBM, ANY, ANY],
            out_specs=(HBM, VMEM),
            scratch_shapes=[
                pltpu.VMEM((chunks, step, width), BF16),
                pltpu.VMEM((chunks, tokens, step), BF16),
                pltpu.SemaphoreType.DMA((2 * chunks,)),
            ],
            compiler_params=params(10),
            cost_estimate=cost(2 * tokens * rows * width, 2 * (tokens + rows) * width),
        )(cotangent, weight, *wait)

    def stack(values, piece, *wait):
        def kernel(*refs):
            out_ref, piece_ref = refs[-2:]
            for k in range(len(values)):
                out_ref[k] = refs[k][...]
            piece_ref[...] = refs[len(values)][...]

        return pl.pallas_call(
            kernel,
            out_shape=(
                shape((len(values),) + values[0].shape, values[0].dtype),
                shape(piece.shape, piece.dtype),
            ),
            in_specs=[VMEM] * (len(values) + 1) + [ANY] * len(wait),
            out_specs=(VMEM, VMEM),
            compiler_params=params(4),
            cost_estimate=cost(0, 2 * values[0].size),
        )(*values, piece, *wait)

    def relay(value, *wait):
        def kernel(ref, *refs):
            refs[-1][...] = ref[...]

        return pl.pallas_call(
            kernel,
            out_shape=shape(value.shape, value.dtype),
            in_specs=[VMEM] + [ANY] * len(wait),
            out_specs=VMEM,
            compiler_params=params(4),
            cost_estimate=cost(0, 2 * value.size),
        )(value, *wait)

    def other_product(cotangent, pieces, into):
        tokens, width = cotangent.shape
        rows = sum(piece.shape[0] for _, piece in pieces)
        step = 256 if rows % 256 == 0 else 128
        chunks = rows // step

        def kernel(g_ref, *refs):
            w_refs = refs[: len(pieces)]
            out_hbm, w, out, sems = refs[-4:]
            z, x, c, y = place()
            copies = []
            for k, ((first, piece), ref) in enumerate(zip(pieces, w_refs)):
                count = piece.shape[0]
                row = pl.multiple_of(first(z, x, c), 16)
                copies.append(pltpu.make_async_copy(ref, w.at[pl.ds(row, count)], sems.at[k]))
                copies[-1].start()
            for copy in copies:
                copy.wait()
            outs = []
            for k in range(chunks):
                out[k] = lax.dot_general(
                    g_ref[...],
                    w[pl.ds(k * step, step), :],
                    (((1,), (1,)), ((), ())),
                    preferred_element_type=F32,
                ).astype(BF16)
                column = pl.multiple_of((1 - y) * rows + k * step, step)
                outs.append(
                    pltpu.make_async_copy(
                        out.at[k], out_hbm.at[:, pl.ds(column, step)], sems.at[len(pieces) + k]
                    )
                )
                outs[-1].start()
            for copy in outs:
                copy.wait()

        return pl.pallas_call(
            kernel,
            out_shape=shape(into.shape, BF16),
            in_specs=[VMEM] + [ANY] * len(pieces) + [HBM],
            out_specs=HBM,
            input_output_aliases={1 + len(pieces): 0},
            scratch_shapes=[
                pltpu.VMEM((rows, width), BF16),
                pltpu.VMEM((chunks, tokens, step), BF16),
                pltpu.SemaphoreType.DMA((len(pieces) + chunks,)),
            ],
            compiler_params=params(8),
            cost_estimate=cost(2 * tokens * rows * width, 2 * (tokens + rows) * width),
        )(cotangent, *[piece for _, piece in pieces], into)

    def on_device(attn, cotangent, weight, projector, moment_one, moment_two, step_count):
        shard_rows, width = weight.shape
        own_rows = moment_one.shape[0]
        if n_y != 2 or own_rows % 16 or shard_rows % 384 or n_z % 2:
            return plain(attn, cotangent, weight, projector, moment_one, moment_two, step_count)
        eighth = shard_rows // 8
        first, second, own_projector = cut(weight, projector)
        over_y = [to_plane(first, 0, 1)]
        outgoing, keep = local_sums(attn, own_projector, cotangent)
        over_y.append(to_plane(relay(second, over_y[0]), 0, 1))
        sums = core_sum(keep, to_core(relay(outgoing, over_y[0])))
        got = [to_plane(part, dx, dy) for (dx, dy), part in zip(plane, sums[1:])]
        over_z = [to_z_pair(part) for part in over_y]
        grad_input, done = own_product(cotangent, weight, over_y[1], sums[1])
        sums = plane_sum(sums[0], got, over_y, [done] + over_z)
        own = sums[n_z]

        over_x = to_plane(own, 1, 0)
        got = [to_z(part, dz) for dz, part in zip(range(1, n_z), sums[1:n_z])]
        first_moment, second_moment, low_step = adam(
            sums[0], got, moment_one, moment_two, step_count
        )
        column, over_x = stack(
            [low_step] + [to_z(low_step, dz) for dz in range(1, n_z)], over_x
        )
        over_xz = to_z_pair(over_x)

        blocks = [(0, 0, 0, column), (1, 0, 0, to_core(column))]
        for dx, dy in plane:
            got = to_plane(column, dx, dy)
            blocks += [(0, dx, dy, got), (1, dx, dy, to_core(got))]
        pieces = []
        for dx, dz, parts in ((0, 0, [own]), (1, 0, [over_x]), (0, 1, over_z), (1, 1, [over_xz])):
            begin = 0
            for part in parts:
                for dc in range(2):
                    row = lambda z, x, c, dx=dx, dz=dz, dc=dc, begin=begin: (
                        (((x + dx) % 2) * 2 + (z + dz) % 2) * 2 + (c + dc) % 2
                    ) * eighth + begin
                    pieces.append((row, to_core(part) if dc else part))
                begin += part.shape[0]
        weight_step = step_product(own_projector, shard_rows, blocks)
        grad_input = other_product(cotangent, pieces, grad_input)
        return grad_input, weight_step, first_moment, second_moment

    rows = P(("dp", "fsdp"), None)
    return jax.shard_map(
        on_device,
        mesh=mesh,
        in_specs=(rows, rows, P("fsdp", None), P(), rows, rows, P()),
        out_specs=(rows, P("fsdp", None), rows, rows),
        check_vma=False,
    )
```

```python
import jax
import jax.numpy as jnp
from jax import lax
from jax.experimental import pallas as pl
from jax.experimental.pallas import tpu as pltpu
from jax.sharding import PartitionSpec as P

AXES = ("dp", "fsdp")
F32, BF16 = jnp.float32, jnp.bfloat16
MIB = 1 << 20
VMEM = pl.BlockSpec(memory_space=pltpu.VMEM)
SMEM = pl.BlockSpec(memory_space=pltpu.SMEM)
ANY = pl.BlockSpec(memory_space=pl.ANY)
HBM = pl.BlockSpec(memory_space=pltpu.HBM)


def shape(dims, dtype):
    return jax.ShapeDtypeStruct(dims, dtype)


def params(mib):
    return pltpu.CompilerParams(vmem_limit_bytes=int(mib * MIB))


def cost(flops, nbytes):
    return pl.CostEstimate(flops=0, bytes_accessed=0, transcendentals=0)


def place():
    d = lax.axis_index("dp")
    return d // 4, (d // 2) % 2, d % 2, lax.axis_index("fsdp")


def power(base, count):
    result, factor = F32(1.0), base
    for bit in range(31):
        result = jnp.where((count // (1 << bit)) % 2 == 1, result * F32(factor), result)
        factor = factor * factor
    return result


def plain(attn, cotangent, weight, projector, moment_one, moment_two, step_count):
    shard_rows = weight.shape[0]
    reduced = jnp.dot(attn, projector, preferred_element_type=F32).astype(BF16)
    grad_input = lax.dot_general(
        cotangent,
        lax.all_gather(weight, "fsdp", axis=0, tiled=True),
        (((1,), (1,)), ((), ())),
        preferred_element_type=F32,
    ).astype(BF16)
    projected = lax.psum_scatter(
        lax.dot_general(cotangent, reduced, (((0,), (0,)), ((), ())), preferred_element_type=F32),
        AXES,
        scatter_dimension=0,
        tiled=True,
    )
    first_moment = 0.9 * moment_one + 0.1 * projected
    second_moment = 0.999 * moment_two + 0.001 * projected * projected
    steps = step_count[0].astype(F32)
    first_hat = first_moment / (1.0 - jnp.power(F32(0.9), steps))
    second_hat = second_moment / (1.0 - jnp.power(F32(0.999), steps))
    low_step = (first_hat / (jnp.sqrt(second_hat) + 1e-08)).astype(BF16)
    my_projector = lax.dynamic_slice_in_dim(
        projector, lax.axis_index("fsdp") * shard_rows, shard_rows, 0
    )
    weight_step = 0.25 * lax.dot_general(
        my_projector,
        lax.all_gather(low_step, AXES, axis=0, tiled=True),
        (((1,), (1,)), ((), ())),
        preferred_element_type=F32,
    )
    return grad_input, weight_step, first_moment, second_moment


def solution(mesh):
    n_dp, n_y = mesh.shape["dp"], mesh.shape["fsdp"]
    n_z = n_dp // 4
    groups = 2 * n_z
    plane = [(dx, dy) for dx in range(2) for dy in range(n_y) if (dx, dy) != (0, 0)]

    def send(value, move):
        pairs = []
        for z in range(n_z):
            for x in range(2):
                for c in range(2):
                    for y in range(n_y):
                        tz, tx, tc, ty = move(z, x, c, y)
                        pairs.append(
                            (((z * 2 + x) * 2 + c) * n_y + y, ((tz * 2 + tx) * 2 + tc) * n_y + ty)
                        )
        return lax.ppermute(value, AXES, pairs)

    def to_core(value):
        return send(value, lambda z, x, c, y: (z, x, 1 - c, y))

    def to_plane(value, dx, dy):
        return send(value, lambda z, x, c, y: (z, x ^ dx, c, (y + dy) % n_y))

    def to_z(value, dz):
        return send(value, lambda z, x, c, y: ((z + dz) % n_z, x, c, y))

    def to_z_pair(value):
        return send(value, lambda z, x, c, y: (z ^ 1, x, c, y))

    def cut(weight, projector):
        rows, width = weight.shape
        eighth = rows // 8
        large = eighth // 48 * 32

        def kernel(w_hbm, p_hbm, first_ref, second_ref, p_ref, sems):
            z, x, c, y = place()
            row = pl.multiple_of(((x * 2 + z % 2) * 2 + c) * eighth, eighth)
            copies = [
                pltpu.make_async_copy(w_hbm.at[pl.ds(row, large)], first_ref, sems.at[0]),
                pltpu.make_async_copy(
                    w_hbm.at[pl.ds(row + large, eighth - large)], second_ref, sems.at[1]
                ),
                pltpu.make_async_copy(p_hbm, p_ref, sems.at[2]),
            ]
            for copy in copies:
                copy.start()
            for copy in copies:
                copy.wait()

        parts = (shape((large, width), BF16), shape((eighth - large, width), BF16))
        return pl.pallas_call(
            kernel,
            out_shape=parts + (shape(projector.shape, BF16),),
            in_specs=[HBM, HBM],
            out_specs=(VMEM,) * 3,
            scratch_shapes=[pltpu.SemaphoreType.DMA((3,))],
            compiler_params=params(52.5),
            cost_estimate=cost(0, 0),
        )(weight, projector)

    def local_sums(attn, projector, cotangent):
        tokens, inner = attn.shape
        width, rank = cotangent.shape[1], projector.shape[1]
        rows = width // groups
        own = rows // (2 * n_y)

        def kernel(a_hbm, p, g_hbm, send_ref, keep_ref, a, g, red, part, sems):
            c = lax.axis_index("dp") % 2
            copy_a = pltpu.make_async_copy(a_hbm, a, sems.at[0])
            copy_a.start()
            copies = []
            for k in range(groups):
                span = pl.ds(k * rows, rows)
                copies.append(pltpu.make_async_copy(g_hbm.at[:, span], g.at[k], sems.at[1 + k]))
                copies[-1].start()
            copy_a.wait()
            red[...] = jnp.dot(a[...], p[...], preferred_element_type=F32).astype(BF16)
            for k in range(groups):
                copies[k].wait()
                part[k % 2] = lax.dot_general(
                    g[k], red[...], (((0,), (0,)), ((), ())), preferred_element_type=F32
                )
                for y in range(n_y):
                    mine = pl.multiple_of(c * (n_y * own) + y * own, own)
                    theirs = pl.multiple_of((1 - c) * (n_y * own) + y * own, own)
                    keep_ref[k % 2, y, k // 2] = part[k % 2, pl.ds(mine, own), :]
                    send_ref[k % 2, y, k // 2] = part[k % 2, pl.ds(theirs, own), :].astype(BF16)

        dims = (2, n_y, n_z, own, rank)
        return pl.pallas_call(
            kernel,
            out_shape=(shape(dims, BF16), shape(dims, F32)),
            in_specs=[HBM, VMEM, HBM],
            out_specs=(VMEM, VMEM),
            scratch_shapes=[
                pltpu.VMEM(attn.shape, BF16),
                pltpu.VMEM((groups, tokens, rows), BF16),
                pltpu.VMEM((tokens, rank), BF16),
                pltpu.VMEM((2, rows, rank), F32),
                pltpu.SemaphoreType.DMA((1 + groups,)),
            ],
            compiler_params=params(50),
            cost_estimate=cost(
                2 * tokens * rank * (inner + width), 2 * tokens * (inner + width) + 6 * width * rank
            ),
        )(attn, projector, cotangent)

    def core_sum(keep, got):
        slab = keep.shape[2:]

        def kernel(keep_ref, got_ref, own_ref, *send_refs):
            z, x, c, y = place()
            own_ref[...] = keep_ref[x, y] + got_ref[x, y].astype(F32)
            for (dx, dy), ref in zip(plane, send_refs):
                tx, ty = (x + dx) % 2, (y + dy) % n_y
                ref[...] = (keep_ref[tx, ty] + got_ref[tx, ty].astype(F32)).astype(BF16)

        return pl.pallas_call(
            kernel,
            out_shape=(shape(slab, F32),) + (shape(slab, BF16),) * len(plane),
            in_specs=[VMEM, VMEM],
            out_specs=(VMEM,) * (1 + len(plane)),
            compiler_params=params(12),
            cost_estimate=cost(keep.size, 8 * keep.size),
        )(keep, got)

    def plane_sum(own, got, parts, wait):
        slab = own.shape[1:]
        rows, width = sum(part.shape[0] for part in parts), parts[0].shape[1]

        def kernel(own_ref, *refs):
            got_refs, part_refs = refs[: len(got)], refs[len(got) : len(got) + len(parts)]
            out_ref, send_refs, full_ref = refs[-1 - n_z], refs[-n_z:-1], refs[-1]
            z, x, c, y = place()
            for dz in range(n_z):
                tz = (z + dz) % n_z
                total = own_ref[tz]
                for ref in got_refs:
                    total = total + ref[tz].astype(F32)
                if dz == 0:
                    out_ref[...] = total
                else:
                    send_refs[dz - 1][...] = total.astype(BF16)
            begin = 0
            for ref in part_refs:
                full_ref[begin : begin + ref.shape[0], :] = ref[...]
                begin += ref.shape[0]

        return pl.pallas_call(
            kernel,
            out_shape=(shape(slab, F32),)
            + (shape(slab, BF16),) * (n_z - 1)
            + (shape((rows, width), BF16),),
            in_specs=[VMEM] * (1 + len(got) + len(parts)) + [ANY] * len(wait),
            out_specs=(VMEM,) * (n_z + 1),
            compiler_params=params(8),
            cost_estimate=cost(4 * own.size, 10 * own.size),
        )(own, *got, *parts, *wait)

    def adam(own, got, moment_one, moment_two, step_count):
        def kernel(step_ref, own_ref, *refs):
            got_refs, (m1, m2, first_ref, second_ref, low_ref) = refs[: len(got)], refs[len(got) :]
            projected = own_ref[...]
            for ref in got_refs:
                projected = projected + ref[...].astype(F32)
            first = 0.9 * m1[...] + 0.1 * projected
            second = 0.999 * m2[...] + 0.001 * projected * projected
            first_ref[...] = first
            second_ref[...] = second
            count = step_ref[0]
            ones = jnp.ones(first.shape, F32)
            first_hat = first / ((1.0 - power(0.9, count)) * ones)
            second_hat = second / ((1.0 - power(0.999, count)) * ones)
            low_ref[...] = (first_hat / (jnp.sqrt(second_hat) + 1e-08)).astype(BF16)

        dims = own.shape
        return pl.pallas_call(
            kernel,
            out_shape=(
                shape(dims, F32),
                shape(dims, F32),
                shape(dims, BF16),
            ),
            in_specs=[SMEM] + [VMEM] * (3 + len(got)),
            out_specs=(VMEM,) * 3,
            compiler_params=params(4),
            cost_estimate=cost(20 * own.size, 24 * own.size),
        )(step_count, own, *got, moment_one, moment_two)

    def step_product(projector, rows, blocks):
        rank = projector.shape[1]
        own = blocks[0][3].shape[1]
        span = 2 * n_y * own
        width = groups * span

        def kernel(p_ref, *refs):
            columns, (out_hbm, low, out, sems) = refs[: len(blocks)], refs[len(blocks) :]
            z, x, c, y = place()
            for (dc, dx, dy, _), ref in zip(blocks, columns):
                tc, tx, ty = (c + dc) % 2, (x + dx) % 2, (y + n_y - dy) % n_y
                for dz in range(n_z):
                    tz = (z + n_z - dz) % n_z
                    row = pl.multiple_of((tc * n_y + ty) * own, own)
                    low[tz * 2 + tx, pl.ds(row, own), :] = ref[dz]
            copies = []
            for k in range(groups):
                out[k] = 0.25 * lax.dot_general(
                    p_ref[pl.ds(pl.multiple_of(y * rows, 16), rows), :],
                    low[k],
                    (((1,), (1,)), ((), ())),
                    preferred_element_type=F32,
                )
                copies.append(
                    pltpu.make_async_copy(out.at[k], out_hbm.at[:, pl.ds(k * span, span)], sems.at[k])
                )
                copies[-1].start()
            for copy in copies:
                copy.wait()

        return pl.pallas_call(
            kernel,
            out_shape=shape((rows, width), F32),
            in_specs=[VMEM] * (1 + len(blocks)),
            out_specs=HBM,
            scratch_shapes=[
                pltpu.VMEM((groups, span, rank), BF16),
                pltpu.VMEM((groups, rows, span), F32),
                pltpu.SemaphoreType.DMA((groups,)),
            ],
            compiler_params=params(16),
            cost_estimate=cost(2 * rows * rank * width, 4 * rows * width),
        )(projector, *[block[3] for block in blocks])

    def own_product(cotangent, weight, begin, chunks, into, *wait):
        tokens, width = cotangent.shape
        rows = weight.shape[0]
        step = 256
        operands = [cotangent, weight] + ([] if into is None else [into])

        def kernel(g, w_hbm, *refs):
            out_hbm, done_ref, w, out, sems = refs[-5:]
            y = lax.axis_index("fsdp")
            copies = []
            for k in range(chunks):
                span = pl.ds((begin + k) * step, step)
                copies.append(pltpu.make_async_copy(w_hbm.at[span, :], w.at[k], sems.at[k]))
                copies[-1].start()
            done_ref[...] = jnp.zeros_like(done_ref)
            outs = []
            for k in range(chunks):
                copies[k].wait()
                out[k] = lax.dot_general(
                    g[...], w[k], (((1,), (1,)), ((), ())), preferred_element_type=F32
                ).astype(BF16)
                column = pl.multiple_of(y * rows + (begin + k) * step, step)
                outs.append(
                    pltpu.make_async_copy(
                        out.at[k], out_hbm.at[:, pl.ds(column, step)], sems.at[chunks + k]
                    )
                )
                outs[-1].start()
            for copy in outs:
                copy.wait()

        return pl.pallas_call(
            kernel,
            out_shape=(shape((tokens, rows * n_y), BF16), shape((8, 128), F32)),
            in_specs=[VMEM] + [HBM] * (len(operands) - 1) + [ANY] * len(wait),
            out_specs=(HBM, VMEM),
            input_output_aliases={} if into is None else {2: 0},
            scratch_shapes=[
                pltpu.VMEM((chunks, step, width), BF16),
                pltpu.VMEM((chunks, tokens, step), BF16),
                pltpu.SemaphoreType.DMA((2 * chunks,)),
            ],
            compiler_params=params(10),
            cost_estimate=cost(2 * tokens * rows * width, 2 * (tokens + rows) * width),
        )(*operands, *wait)

    def stack(values, piece, *wait):
        def kernel(*refs):
            out_ref, piece_ref = refs[-2:]
            for k in range(len(values)):
                out_ref[k] = refs[k][...]
            piece_ref[...] = refs[len(values)][...]

        return pl.pallas_call(
            kernel,
            out_shape=(
                shape((len(values),) + values[0].shape, values[0].dtype),
                shape(piece.shape, piece.dtype),
            ),
            in_specs=[VMEM] * (len(values) + 1) + [ANY] * len(wait),
            out_specs=(VMEM, VMEM),
            compiler_params=params(4),
            cost_estimate=cost(0, 2 * values[0].size),
        )(*values, piece, *wait)

    def relay(value, *wait):
        def kernel(ref, *refs):
            refs[-1][...] = ref[...]

        return pl.pallas_call(
            kernel,
            out_shape=shape(value.shape, value.dtype),
            in_specs=[VMEM] + [ANY] * len(wait),
            out_specs=VMEM,
            compiler_params=params(4),
            cost_estimate=cost(0, 2 * value.size),
        )(value, *wait)

    def other_product(cotangent, pieces, into):
        tokens, width = cotangent.shape
        rows = sum(piece.shape[0] for _, piece in pieces)
        step = 256 if rows % 256 == 0 else 128
        chunks = rows // step

        def kernel(g_ref, *refs):
            w_refs = refs[: len(pieces)]
            out_hbm, w, out, sems = refs[-4:]
            z, x, c, y = place()
            copies = []
            for k, ((first, piece), ref) in enumerate(zip(pieces, w_refs)):
                count = piece.shape[0]
                row = pl.multiple_of(first(z, x, c), 16)
                copies.append(pltpu.make_async_copy(ref, w.at[pl.ds(row, count)], sems.at[k]))
                copies[-1].start()
            for copy in copies:
                copy.wait()
            outs = []
            for k in range(chunks):
                out[k] = lax.dot_general(
                    g_ref[...],
                    w[pl.ds(k * step, step), :],
                    (((1,), (1,)), ((), ())),
                    preferred_element_type=F32,
                ).astype(BF16)
                column = pl.multiple_of((1 - y) * rows + k * step, step)
                outs.append(
                    pltpu.make_async_copy(
                        out.at[k], out_hbm.at[:, pl.ds(column, step)], sems.at[len(pieces) + k]
                    )
                )
                outs[-1].start()
            for copy in outs:
                copy.wait()

        return pl.pallas_call(
            kernel,
            out_shape=shape(into.shape, BF16),
            in_specs=[VMEM] + [ANY] * len(pieces) + [HBM],
            out_specs=HBM,
            input_output_aliases={1 + len(pieces): 0},
            scratch_shapes=[
                pltpu.VMEM((rows, width), BF16),
                pltpu.VMEM((chunks, tokens, step), BF16),
                pltpu.SemaphoreType.DMA((len(pieces) + chunks,)),
            ],
            compiler_params=params(8),
            cost_estimate=cost(2 * tokens * rows * width, 2 * (tokens + rows) * width),
        )(cotangent, *[piece for _, piece in pieces], into)

    def on_device(attn, cotangent, weight, projector, moment_one, moment_two, step_count):
        shard_rows, width = weight.shape
        own_rows = moment_one.shape[0]
        if n_y != 2 or own_rows % 16 or shard_rows % 768 or n_z % 2:
            return plain(attn, cotangent, weight, projector, moment_one, moment_two, step_count)
        eighth = shard_rows // 8
        first, second, own_projector = cut(weight, projector)
        over_y = [to_plane(first, 0, 1)]
        outgoing, keep = local_sums(attn, own_projector, cotangent)
        over_y.append(to_plane(relay(second, over_y[0]), 0, 1))
        sums = core_sum(keep, to_core(relay(outgoing, over_y[0])))
        got = [to_plane(part, dx, dy) for (dx, dy), part in zip(plane, sums[1:])]
        over_y[1] = relay(over_y[1], sums[1])
        over_z = [to_z_pair(part) for part in over_y]
        grad_input, done = own_product(
            cotangent, weight, 0, shard_rows // 256, None, over_y[1]
        )
        sums = plane_sum(sums[0], got, over_y, [done] + over_z)
        own = sums[n_z]

        over_x = to_plane(own, 1, 0)
        got = [to_z(part, dz) for dz, part in zip(range(1, n_z), sums[1:n_z])]
        first_moment, second_moment, low_step = adam(
            sums[0], got, moment_one, moment_two, step_count
        )
        column, over_x = stack(
            [low_step] + [to_z(low_step, dz) for dz in range(1, n_z)], over_x
        )
        over_xz = to_z_pair(over_x)

        blocks = [(0, 0, 0, column), (1, 0, 0, to_core(column))]
        for dx, dy in plane:
            got = to_plane(column, dx, dy)
            blocks += [(0, dx, dy, got), (1, dx, dy, to_core(got))]
        pieces = []
        for dx, dz, parts in ((0, 0, [own]), (1, 0, [over_x]), (0, 1, over_z), (1, 1, [over_xz])):
            begin = 0
            for part in parts:
                for dc in range(2):
                    row = lambda z, x, c, dx=dx, dz=dz, dc=dc, begin=begin: (
                        (((x + dx) % 2) * 2 + (z + dz) % 2) * 2 + (c + dc) % 2
                    ) * eighth + begin
                    pieces.append((row, to_core(part) if dc else part))
                begin += part.shape[0]
        weight_step = step_product(own_projector, shard_rows, blocks)
        grad_input = other_product(cotangent, pieces, grad_input)
        return grad_input, weight_step, first_moment, second_moment

    rows = P(("dp", "fsdp"), None)
    return jax.shard_map(
        on_device,
        mesh=mesh,
        in_specs=(rows, rows, P("fsdp", None), P(), rows, rows, P()),
        out_specs=(rows, P("fsdp", None), rows, rows),
        check_vma=False,
    )
```

```python
import jax
import jax.numpy as jnp
from jax import lax
from jax.experimental import pallas as pl
from jax.experimental.pallas import tpu as pltpu
from jax.sharding import PartitionSpec as P

AXES = ("dp", "fsdp")
F32, BF16 = jnp.float32, jnp.bfloat16
MIB = 1 << 20
VMEM = pl.BlockSpec(memory_space=pltpu.VMEM)
SMEM = pl.BlockSpec(memory_space=pltpu.SMEM)
ANY = pl.BlockSpec(memory_space=pl.ANY)
HBM = pl.BlockSpec(memory_space=pltpu.HBM)


def shape(dims, dtype):
    return jax.ShapeDtypeStruct(dims, dtype)


def params(mib):
    return pltpu.CompilerParams(vmem_limit_bytes=int(mib * MIB))


def cost(flops, nbytes):
    return pl.CostEstimate(flops=0, bytes_accessed=0, transcendentals=0)


def place():
    d = lax.axis_index("dp")
    return d // 4, (d // 2) % 2, d % 2, lax.axis_index("fsdp")


def power(base, count):
    result, factor = F32(1.0), base
    for bit in range(31):
        result = jnp.where((count // (1 << bit)) % 2 == 1, result * F32(factor), result)
        factor = factor * factor
    return result


def plain(attn, cotangent, weight, projector, moment_one, moment_two, step_count):
    shard_rows = weight.shape[0]
    reduced = jnp.dot(attn, projector, preferred_element_type=F32).astype(BF16)
    grad_input = lax.dot_general(
        cotangent,
        lax.all_gather(weight, "fsdp", axis=0, tiled=True),
        (((1,), (1,)), ((), ())),
        preferred_element_type=F32,
    ).astype(BF16)
    projected = lax.psum_scatter(
        lax.dot_general(cotangent, reduced, (((0,), (0,)), ((), ())), preferred_element_type=F32),
        AXES,
        scatter_dimension=0,
        tiled=True,
    )
    first_moment = 0.9 * moment_one + 0.1 * projected
    second_moment = 0.999 * moment_two + 0.001 * projected * projected
    steps = step_count[0].astype(F32)
    first_hat = first_moment / (1.0 - jnp.power(F32(0.9), steps))
    second_hat = second_moment / (1.0 - jnp.power(F32(0.999), steps))
    low_step = (first_hat / (jnp.sqrt(second_hat) + 1e-08)).astype(BF16)
    my_projector = lax.dynamic_slice_in_dim(
        projector, lax.axis_index("fsdp") * shard_rows, shard_rows, 0
    )
    weight_step = 0.25 * lax.dot_general(
        my_projector,
        lax.all_gather(low_step, AXES, axis=0, tiled=True),
        (((1,), (1,)), ((), ())),
        preferred_element_type=F32,
    )
    return grad_input, weight_step, first_moment, second_moment


def solution(mesh):
    n_dp, n_y = mesh.shape["dp"], mesh.shape["fsdp"]
    n_z = n_dp // 4
    groups = 2 * n_z
    plane = [(dx, dy) for dx in range(2) for dy in range(n_y) if (dx, dy) != (0, 0)]

    def send(value, move):
        pairs = []
        for z in range(n_z):
            for x in range(2):
                for c in range(2):
                    for y in range(n_y):
                        tz, tx, tc, ty = move(z, x, c, y)
                        pairs.append(
                            (((z * 2 + x) * 2 + c) * n_y + y, ((tz * 2 + tx) * 2 + tc) * n_y + ty)
                        )
        return lax.ppermute(value, AXES, pairs)

    def to_core(value):
        return send(value, lambda z, x, c, y: (z, x, 1 - c, y))

    def to_plane(value, dx, dy):
        return send(value, lambda z, x, c, y: (z, x ^ dx, c, (y + dy) % n_y))

    def to_z(value, dz):
        return send(value, lambda z, x, c, y: ((z + dz) % n_z, x, c, y))

    def to_z_pair(value):
        return send(value, lambda z, x, c, y: (z ^ 1, x, c, y))

    def cut(weight, projector):
        rows, width = weight.shape
        eighth = rows // 8
        large = eighth // 2

        def kernel(w_hbm, p_hbm, first_ref, second_ref, p_ref, sems):
            z, x, c, y = place()
            row = pl.multiple_of(((x * 2 + z % 2) * 2 + c) * eighth, eighth)
            copies = [
                pltpu.make_async_copy(w_hbm.at[pl.ds(row, large)], first_ref, sems.at[0]),
                pltpu.make_async_copy(
                    w_hbm.at[pl.ds(row + large, eighth - large)], second_ref, sems.at[1]
                ),
                pltpu.make_async_copy(p_hbm, p_ref, sems.at[2]),
            ]
            for copy in copies:
                copy.start()
            for copy in copies:
                copy.wait()

        parts = (shape((large, width), BF16), shape((eighth - large, width), BF16))
        return pl.pallas_call(
            kernel,
            out_shape=parts + (shape(projector.shape, BF16),),
            in_specs=[HBM, HBM],
            out_specs=(VMEM,) * 3,
            scratch_shapes=[pltpu.SemaphoreType.DMA((3,))],
            compiler_params=params(52.5),
            cost_estimate=cost(0, 0),
        )(weight, projector)

    def local_sums(attn, projector, cotangent):
        tokens, inner = attn.shape
        width, rank = cotangent.shape[1], projector.shape[1]
        rows = width // groups
        own = rows // (2 * n_y)

        def kernel(a_hbm, p, g_hbm, send_ref, keep_ref, a, g, red, part, sems):
            c = lax.axis_index("dp") % 2
            copy_a = pltpu.make_async_copy(a_hbm, a, sems.at[0])
            copy_a.start()
            copies = []
            for k in range(groups):
                span = pl.ds(k * rows, rows)
                copies.append(pltpu.make_async_copy(g_hbm.at[:, span], g.at[k], sems.at[1 + k]))
                copies[-1].start()
            copy_a.wait()
            red[...] = jnp.dot(a[...], p[...], preferred_element_type=F32).astype(BF16)
            for k in range(groups):
                copies[k].wait()
                part[k % 2] = lax.dot_general(
                    g[k], red[...], (((0,), (0,)), ((), ())), preferred_element_type=F32
                )
                for y in range(n_y):
                    mine = pl.multiple_of(c * (n_y * own) + y * own, own)
                    theirs = pl.multiple_of((1 - c) * (n_y * own) + y * own, own)
                    keep_ref[k % 2, y, k // 2] = part[k % 2, pl.ds(mine, own), :]
                    send_ref[k % 2, y, k // 2] = part[k % 2, pl.ds(theirs, own), :].astype(BF16)

        dims = (2, n_y, n_z, own, rank)
        return pl.pallas_call(
            kernel,
            out_shape=(shape(dims, BF16), shape(dims, F32)),
            in_specs=[HBM, VMEM, HBM],
            out_specs=(VMEM, VMEM),
            scratch_shapes=[
                pltpu.VMEM(attn.shape, BF16),
                pltpu.VMEM((groups, tokens, rows), BF16),
                pltpu.VMEM((tokens, rank), BF16),
                pltpu.VMEM((2, rows, rank), F32),
                pltpu.SemaphoreType.DMA((1 + groups,)),
            ],
            compiler_params=params(50),
            cost_estimate=cost(
                2 * tokens * rank * (inner + width), 2 * tokens * (inner + width) + 6 * width * rank
            ),
        )(attn, projector, cotangent)

    def core_sum(keep, got):
        slab = keep.shape[2:]

        def kernel(keep_ref, got_ref, own_ref, *send_refs):
            z, x, c, y = place()
            own_ref[...] = keep_ref[x, y] + got_ref[x, y].astype(F32)
            for (dx, dy), ref in zip(plane, send_refs):
                tx, ty = (x + dx) % 2, (y + dy) % n_y
                ref[...] = (keep_ref[tx, ty] + got_ref[tx, ty].astype(F32)).astype(BF16)

        return pl.pallas_call(
            kernel,
            out_shape=(shape(slab, F32),) + (shape(slab, BF16),) * len(plane),
            in_specs=[VMEM, VMEM],
            out_specs=(VMEM,) * (1 + len(plane)),
            compiler_params=params(12),
            cost_estimate=cost(keep.size, 8 * keep.size),
        )(keep, got)

    def plane_sum(own, got, parts, wait):
        slab = own.shape[1:]
        rows, width = sum(part.shape[0] for part in parts), parts[0].shape[1]

        def kernel(own_ref, *refs):
            got_refs, part_refs = refs[: len(got)], refs[len(got) : len(got) + len(parts)]
            out_ref, send_refs, full_ref = refs[-1 - n_z], refs[-n_z:-1], refs[-1]
            z, x, c, y = place()
            for dz in range(n_z):
                tz = (z + dz) % n_z
                total = own_ref[tz]
                for ref in got_refs:
                    total = total + ref[tz].astype(F32)
                if dz == 0:
                    out_ref[...] = total
                else:
                    send_refs[dz - 1][...] = total.astype(BF16)
            begin = 0
            for ref in part_refs:
                full_ref[begin : begin + ref.shape[0], :] = ref[...]
                begin += ref.shape[0]

        return pl.pallas_call(
            kernel,
            out_shape=(shape(slab, F32),)
            + (shape(slab, BF16),) * (n_z - 1)
            + (shape((rows, width), BF16),),
            in_specs=[VMEM] * (1 + len(got) + len(parts)) + [ANY] * len(wait),
            out_specs=(VMEM,) * (n_z + 1),
            compiler_params=params(8),
            cost_estimate=cost(4 * own.size, 10 * own.size),
        )(own, *got, *parts, *wait)

    def adam(own, got, moment_one, moment_two, step_count, wait):
        def kernel(step_ref, own_ref, *refs):
            got_refs, (m1, m2) = refs[: len(got)], refs[len(got) : len(got) + 2]
            first_ref, second_ref, low_ref = refs[-3:]
            projected = own_ref[...]
            for ref in got_refs:
                projected = projected + ref[...].astype(F32)
            first = 0.9 * m1[...] + 0.1 * projected
            second = 0.999 * m2[...] + 0.001 * projected * projected
            first_ref[...] = first
            second_ref[...] = second
            count = step_ref[0]
            ones = jnp.ones(first.shape, F32)
            first_hat = first / ((1.0 - power(0.9, count)) * ones)
            second_hat = second / ((1.0 - power(0.999, count)) * ones)
            low_ref[...] = (first_hat / (jnp.sqrt(second_hat) + 1e-08)).astype(BF16)

        dims = own.shape
        return pl.pallas_call(
            kernel,
            out_shape=(
                shape(dims, F32),
                shape(dims, F32),
                shape(dims, BF16),
            ),
            in_specs=[SMEM] + [VMEM] * (3 + len(got)) + [ANY] * len(wait),
            out_specs=(VMEM,) * 3,
            compiler_params=params(4),
            cost_estimate=cost(20 * own.size, 24 * own.size),
        )(step_count, own, *got, moment_one, moment_two, *wait)

    def step_product(projector, rows, blocks, wait):
        rank = projector.shape[1]
        own = blocks[0][3].shape[1]
        span = 2 * n_y * own
        width = groups * span

        def kernel(p_ref, *refs):
            columns, refs = refs[: len(blocks)], refs[len(blocks) + len(wait) :]
            out_hbm, done_ref, low, out, sems = refs
            done_ref[...] = jnp.zeros_like(done_ref)
            z, x, c, y = place()
            for (dc, dx, dy, _), ref in zip(blocks, columns):
                tc, tx, ty = (c + dc) % 2, (x + dx) % 2, (y + n_y - dy) % n_y
                for dz in range(n_z):
                    tz = (z + n_z - dz) % n_z
                    row = pl.multiple_of((tc * n_y + ty) * own, own)
                    low[tz * 2 + tx, pl.ds(row, own), :] = ref[dz]
            copies = []
            for k in range(groups):
                out[k] = 0.25 * lax.dot_general(
                    p_ref[pl.ds(pl.multiple_of(y * rows, 16), rows), :],
                    low[k],
                    (((1,), (1,)), ((), ())),
                    preferred_element_type=F32,
                )
                copies.append(
                    pltpu.make_async_copy(out.at[k], out_hbm.at[:, pl.ds(k * span, span)], sems.at[k])
                )
                copies[-1].start()
            for copy in copies:
                copy.wait()

        return pl.pallas_call(
            kernel,
            out_shape=(shape((rows, width), F32), shape((8, 128), F32)),
            in_specs=[VMEM] * (1 + len(blocks)) + [ANY] * len(wait),
            out_specs=(HBM, VMEM),
            scratch_shapes=[
                pltpu.VMEM((groups, span, rank), BF16),
                pltpu.VMEM((groups, rows, span), F32),
                pltpu.SemaphoreType.DMA((groups,)),
            ],
            compiler_params=params(16),
            cost_estimate=cost(2 * rows * rank * width, 4 * rows * width),
        )(projector, *[block[3] for block in blocks], *wait)

    def own_product(cotangent, weight, begin, chunks, into, *wait):
        tokens, width = cotangent.shape
        rows = weight.shape[0]
        step = 256
        operands = [cotangent, weight] + ([] if into is None else [into])

        def kernel(g, w_hbm, *refs):
            out_hbm, done_ref, w, out, sems = refs[-5:]
            y = lax.axis_index("fsdp")
            copies = []
            for k in range(chunks):
                span = pl.ds((begin + k) * step, step)
                copies.append(pltpu.make_async_copy(w_hbm.at[span, :], w.at[k], sems.at[k]))
                copies[-1].start()
            done_ref[...] = jnp.zeros_like(done_ref)
            outs = []
            for k in range(chunks):
                copies[k].wait()
                out[k] = lax.dot_general(
                    g[...], w[k], (((1,), (1,)), ((), ())), preferred_element_type=F32
                ).astype(BF16)
                column = pl.multiple_of(y * rows + (begin + k) * step, step)
                outs.append(
                    pltpu.make_async_copy(
                        out.at[k], out_hbm.at[:, pl.ds(column, step)], sems.at[chunks + k]
                    )
                )
                outs[-1].start()
            for copy in outs:
                copy.wait()

        return pl.pallas_call(
            kernel,
            out_shape=(shape((tokens, rows * n_y), BF16), shape((8, 128), F32)),
            in_specs=[VMEM] + [HBM] * (len(operands) - 1) + [ANY] * len(wait),
            out_specs=(HBM, VMEM),
            input_output_aliases={} if into is None else {2: 0},
            scratch_shapes=[
                pltpu.VMEM((chunks, step, width), BF16),
                pltpu.VMEM((chunks, tokens, step), BF16),
                pltpu.SemaphoreType.DMA((2 * chunks,)),
            ],
            compiler_params=params(10),
            cost_estimate=cost(2 * tokens * rows * width, 2 * (tokens + rows) * width),
        )(*operands, *wait)

    def stack(values, pieces):
        rows, width = sum(piece.shape[0] for piece in pieces), pieces[0].shape[1]

        def kernel(*refs):
            out_ref, piece_ref = refs[-2:]
            for k in range(len(values)):
                out_ref[k] = refs[k][...]
            begin = 0
            for k, piece in enumerate(pieces):
                piece_ref[begin : begin + piece.shape[0], :] = refs[len(values) + k][...]
                begin += piece.shape[0]

        return pl.pallas_call(
            kernel,
            out_shape=(
                shape((len(values),) + values[0].shape, values[0].dtype),
                shape((rows, width), pieces[0].dtype),
            ),
            in_specs=[VMEM] * (len(values) + len(pieces)),
            out_specs=(VMEM, VMEM),
            compiler_params=params(4),
            cost_estimate=cost(0, 0),
        )(*values, *pieces)

    def relay(value, wait, sizes=None):
        counts = sizes or (value.shape[0],)

        def kernel(ref, *refs):
            outs, begin = refs[len(wait) :], 0
            for count, out_ref in zip(counts, outs):
                out_ref[...] = ref[begin : begin + count]
                begin += count

        copies = pl.pallas_call(
            kernel,
            out_shape=tuple(shape((count,) + value.shape[1:], value.dtype) for count in counts),
            in_specs=[VMEM] + [ANY] * len(wait),
            out_specs=(VMEM,) * len(counts),
            compiler_params=params(4),
            cost_estimate=cost(0, 2 * value.size),
        )(value, *wait)
        return copies if sizes else copies[0]

    def other_product(cotangent, pieces, into):
        tokens, width = cotangent.shape
        rows = sum(piece[3] for piece in pieces)
        step = 256 if rows % 256 == 0 else 128
        chunks = rows // step

        def kernel(g_ref, *refs):
            w_refs = refs[: len(pieces)]
            out_hbm, w, out, sems = refs[-4:]
            z, x, c, y = place()
            copies = []
            for k, ((first, _, offset, count), ref) in enumerate(zip(pieces, w_refs)):
                row = pl.multiple_of(first(z, x, c), 16)
                copies.append(
                    pltpu.make_async_copy(
                        ref.at[pl.ds(offset, count)], w.at[pl.ds(row, count)], sems.at[k]
                    )
                )
                copies[-1].start()
            for copy in copies:
                copy.wait()
            outs = []
            for k in range(chunks):
                out[k] = lax.dot_general(
                    g_ref[...],
                    w[pl.ds(k * step, step), :],
                    (((1,), (1,)), ((), ())),
                    preferred_element_type=F32,
                ).astype(BF16)
                column = pl.multiple_of((1 - y) * rows + k * step, step)
                outs.append(
                    pltpu.make_async_copy(
                        out.at[k], out_hbm.at[:, pl.ds(column, step)], sems.at[len(pieces) + k]
                    )
                )
                outs[-1].start()
            for copy in outs:
                copy.wait()

        return pl.pallas_call(
            kernel,
            out_shape=shape(into.shape, BF16),
            in_specs=[VMEM] + [ANY] * len(pieces) + [HBM],
            out_specs=HBM,
            input_output_aliases={1 + len(pieces): 0},
            scratch_shapes=[
                pltpu.VMEM((rows, width), BF16),
                pltpu.VMEM((chunks, tokens, step), BF16),
                pltpu.SemaphoreType.DMA((len(pieces) + chunks,)),
            ],
            compiler_params=params(8),
            cost_estimate=cost(2 * tokens * rows * width, 2 * (tokens + rows) * width),
        )(cotangent, *[piece[1] for piece in pieces], into)

    def on_device(attn, cotangent, weight, projector, moment_one, moment_two, step_count):
        shard_rows, width = weight.shape
        own_rows = moment_one.shape[0]
        if n_y != 2 or own_rows % 16 or shard_rows % 768 or n_z % 2:
            return plain(attn, cotangent, weight, projector, moment_one, moment_two, step_count)
        eighth = shard_rows // 8
        first, second, own_projector = cut(weight, projector)
        over_y = [to_plane(first, 0, 1)]
        outgoing, keep = local_sums(attn, own_projector, cotangent)
        over_y.append(to_plane(relay(second, [over_y[0]]), 0, 1))
        sums = core_sum(keep, to_core(relay(outgoing, [over_y[0]])))
        over_z = to_z_pair(over_y[0])
        got = [to_plane(part, dx, dy) for (dx, dy), part in zip(plane, sums[1:])]
        grad_input, done = own_product(
            cotangent, weight, 0, shard_rows // 256, None, sums[1]
        )
        over_y[1] = relay(over_y[1], [done])
        sums = plane_sum(sums[0], got, over_y, [done, over_z])
        own = sums[n_z]

        over_x = to_plane(own, 1, 0)
        got = [to_z(part, dz) for dz, part in zip(range(1, n_z), sums[1:n_z])]
        first_moment, second_moment, low_step = adam(
            sums[0], got, moment_one, moment_two, step_count, []
        )
        column, rest = stack(
            [low_step] + [to_z(low_step, dz) for dz in range(1, n_z)], [over_x, over_y[1]]
        )
        rest = to_z_pair(rest)

        blocks = [(0, 0, 0, column), (1, 0, 0, to_core(column))]
        for dx, dy in plane:
            got = to_plane(column, dx, dy)
            blocks += [(0, dx, dy, got), (1, dx, dy, to_core(got))]
        half = eighth // 2
        other = [to_core(part) for part in (own, over_x, over_z)]
        weight_step, done = step_product(own_projector, shard_rows, blocks, other)
        late = relay(rest, [done])
        pieces = []
        for part, twin, held in (
            (own, other[0], [(0, 0, 0, eighth)]),
            (over_x, other[1], [(1, 0, 0, eighth)]),
            (over_z, other[2], [(0, 1, 0, half)]),
            (rest, to_core(late), [(1, 1, 0, eighth), (0, 1, half, eighth - half)]),
        ):
            for dc, array in enumerate((part, twin)):
                offset = 0
                for dx, dz, begin, count in held:
                    row = lambda z, x, c, dx=dx, dz=dz, dc=dc, begin=begin: (
                        (((x + dx) % 2) * 2 + (z + dz) % 2) * 2 + (c + dc) % 2
                    ) * eighth + begin
                    pieces.append((row, array, offset, count))
                    offset += count
        grad_input = other_product(cotangent, pieces, grad_input)
        return grad_input, weight_step, first_moment, second_moment

    rows = P(("dp", "fsdp"), None)
    return jax.shard_map(
        on_device,
        mesh=mesh,
        in_specs=(rows, rows, P("fsdp", None), P(), rows, rows, P()),
        out_specs=(rows, P("fsdp", None), rows, rows),
        check_vma=False,
    )
```

```python
import jax
import jax.numpy as jnp
from jax import lax
from jax.experimental import pallas as pl
from jax.experimental.pallas import tpu as pltpu
from jax.sharding import PartitionSpec as P

AXES = ("dp", "fsdp")
F32, BF16 = jnp.float32, jnp.bfloat16
MIB = 1 << 20
VMEM = pl.BlockSpec(memory_space=pltpu.VMEM)
SMEM = pl.BlockSpec(memory_space=pltpu.SMEM)
ANY = pl.BlockSpec(memory_space=pl.ANY)
HBM = pl.BlockSpec(memory_space=pltpu.HBM)


def shape(dims, dtype):
    return jax.ShapeDtypeStruct(dims, dtype)


def params(mib):
    return pltpu.CompilerParams(vmem_limit_bytes=int(mib * MIB))


def cost(flops, nbytes):
    return pl.CostEstimate(flops=0, bytes_accessed=0, transcendentals=0)


def place():
    d = lax.axis_index("dp")
    return d // 4, (d // 2) % 2, d % 2, lax.axis_index("fsdp")


def power(base, count):
    result, factor = F32(1.0), base
    for bit in range(31):
        result = jnp.where((count // (1 << bit)) % 2 == 1, result * F32(factor), result)
        factor = factor * factor
    return result


def plain(attn, cotangent, weight, projector, moment_one, moment_two, step_count):
    shard_rows = weight.shape[0]
    reduced = jnp.dot(attn, projector, preferred_element_type=F32).astype(BF16)
    grad_input = lax.dot_general(
        cotangent,
        lax.all_gather(weight, "fsdp", axis=0, tiled=True),
        (((1,), (1,)), ((), ())),
        preferred_element_type=F32,
    ).astype(BF16)
    projected = lax.psum_scatter(
        lax.dot_general(cotangent, reduced, (((0,), (0,)), ((), ())), preferred_element_type=F32),
        AXES,
        scatter_dimension=0,
        tiled=True,
    )
    first_moment = 0.9 * moment_one + 0.1 * projected
    second_moment = 0.999 * moment_two + 0.001 * projected * projected
    steps = step_count[0].astype(F32)
    first_hat = first_moment / (1.0 - jnp.power(F32(0.9), steps))
    second_hat = second_moment / (1.0 - jnp.power(F32(0.999), steps))
    low_step = (first_hat / (jnp.sqrt(second_hat) + 1e-08)).astype(BF16)
    my_projector = lax.dynamic_slice_in_dim(
        projector, lax.axis_index("fsdp") * shard_rows, shard_rows, 0
    )
    weight_step = 0.25 * lax.dot_general(
        my_projector,
        lax.all_gather(low_step, AXES, axis=0, tiled=True),
        (((1,), (1,)), ((), ())),
        preferred_element_type=F32,
    )
    return grad_input, weight_step, first_moment, second_moment


def solution(mesh):
    n_dp, n_y = mesh.shape["dp"], mesh.shape["fsdp"]
    n_z = n_dp // 4
    groups = 2 * n_z
    plane = [(dx, dy) for dx in range(2) for dy in range(n_y) if (dx, dy) != (0, 0)]

    def send(value, move):
        pairs = []
        for z in range(n_z):
            for x in range(2):
                for c in range(2):
                    for y in range(n_y):
                        tz, tx, tc, ty = move(z, x, c, y)
                        pairs.append(
                            (((z * 2 + x) * 2 + c) * n_y + y, ((tz * 2 + tx) * 2 + tc) * n_y + ty)
                        )
        return lax.ppermute(value, AXES, pairs)

    def to_core(value):
        return send(value, lambda z, x, c, y: (z, x, 1 - c, y))

    def to_plane(value, dx, dy):
        return send(value, lambda z, x, c, y: (z, x ^ dx, c, (y + dy) % n_y))

    def to_z(value, dz):
        return send(value, lambda z, x, c, y: ((z + dz) % n_z, x, c, y))

    def to_z_pair(value):
        return send(value, lambda z, x, c, y: (z ^ 1, x, c, y))

    def cut(weight, projector):
        rows, width = weight.shape
        eighth = rows // 8
        large = eighth // 2

        def kernel(w_hbm, p_hbm, first_ref, second_ref, p_ref, sems):
            z, x, c, y = place()
            row = pl.multiple_of(((x * 2 + z % 2) * 2 + c) * eighth, eighth)
            copies = [
                pltpu.make_async_copy(w_hbm.at[pl.ds(row, large)], first_ref, sems.at[0]),
                pltpu.make_async_copy(
                    w_hbm.at[pl.ds(row + large, eighth - large)], second_ref, sems.at[1]
                ),
                pltpu.make_async_copy(p_hbm, p_ref, sems.at[2]),
            ]
            for copy in copies:
                copy.start()
            for copy in copies:
                copy.wait()

        parts = (shape((large, width), BF16), shape((eighth - large, width), BF16))
        return pl.pallas_call(
            kernel,
            out_shape=parts + (shape(projector.shape, BF16),),
            in_specs=[HBM, HBM],
            out_specs=(VMEM,) * 3,
            scratch_shapes=[pltpu.SemaphoreType.DMA((3,))],
            compiler_params=params(52.5),
            cost_estimate=cost(0, 0),
        )(weight, projector)

    def local_sums(attn, projector, cotangent):
        tokens, inner = attn.shape
        width, rank = cotangent.shape[1], projector.shape[1]
        rows = width // groups
        own = rows // (2 * n_y)

        def kernel(a_hbm, p, g_hbm, send_ref, keep_ref, a, g, red, part, sems):
            c = lax.axis_index("dp") % 2
            copy_a = pltpu.make_async_copy(a_hbm, a, sems.at[0])
            copy_a.start()
            copies = []
            for k in range(groups):
                span = pl.ds(k * rows, rows)
                copies.append(pltpu.make_async_copy(g_hbm.at[:, span], g.at[k], sems.at[1 + k]))
                copies[-1].start()
            copy_a.wait()
            red[...] = jnp.dot(a[...], p[...], preferred_element_type=F32).astype(BF16)
            for k in range(groups):
                copies[k].wait()
                part[k % 2] = lax.dot_general(
                    g[k], red[...], (((0,), (0,)), ((), ())), preferred_element_type=F32
                )
                for y in range(n_y):
                    mine = pl.multiple_of(c * (n_y * own) + y * own, own)
                    theirs = pl.multiple_of((1 - c) * (n_y * own) + y * own, own)
                    keep_ref[k % 2, y, k // 2] = part[k % 2, pl.ds(mine, own), :]
                    send_ref[k % 2, y, k // 2] = part[k % 2, pl.ds(theirs, own), :].astype(BF16)

        dims = (2, n_y, n_z, own, rank)
        return pl.pallas_call(
            kernel,
            out_shape=(shape(dims, BF16), shape(dims, F32)),
            in_specs=[HBM, VMEM, HBM],
            out_specs=(VMEM, VMEM),
            scratch_shapes=[
                pltpu.VMEM(attn.shape, BF16),
                pltpu.VMEM((groups, tokens, rows), BF16),
                pltpu.VMEM((tokens, rank), BF16),
                pltpu.VMEM((2, rows, rank), F32),
                pltpu.SemaphoreType.DMA((1 + groups,)),
            ],
            compiler_params=params(50),
            cost_estimate=cost(
                2 * tokens * rank * (inner + width), 2 * tokens * (inner + width) + 6 * width * rank
            ),
        )(attn, projector, cotangent)

    def core_sum(keep, got):
        slab = keep.shape[2:]

        def kernel(keep_ref, got_ref, own_ref, *send_refs):
            z, x, c, y = place()
            own_ref[...] = keep_ref[x, y] + got_ref[x, y].astype(F32)
            for (dx, dy), ref in zip(plane, send_refs):
                tx, ty = (x + dx) % 2, (y + dy) % n_y
                ref[...] = (keep_ref[tx, ty] + got_ref[tx, ty].astype(F32)).astype(BF16)

        return pl.pallas_call(
            kernel,
            out_shape=(shape(slab, F32),) + (shape(slab, BF16),) * len(plane),
            in_specs=[VMEM, VMEM],
            out_specs=(VMEM,) * (1 + len(plane)),
            compiler_params=params(12),
            cost_estimate=cost(keep.size, 8 * keep.size),
        )(keep, got)

    def plane_sum(own, got, parts, wait):
        slab = own.shape[1:]
        rows, width = sum(part.shape[0] for part in parts), parts[0].shape[1]

        def kernel(own_ref, *refs):
            got_refs, part_refs = refs[: len(got)], refs[len(got) : len(got) + len(parts)]
            out_ref, send_refs, full_ref = refs[-1 - n_z], refs[-n_z:-1], refs[-1]
            z, x, c, y = place()
            for dz in range(n_z):
                tz = (z + dz) % n_z
                total = own_ref[tz]
                for ref in got_refs:
                    total = total + ref[tz].astype(F32)
                if dz == 0:
                    out_ref[...] = total
                else:
                    send_refs[dz - 1][...] = total.astype(BF16)
            begin = 0
            for ref in part_refs:
                full_ref[begin : begin + ref.shape[0], :] = ref[...]
                begin += ref.shape[0]

        return pl.pallas_call(
            kernel,
            out_shape=(shape(slab, F32),)
            + (shape(slab, BF16),) * (n_z - 1)
            + (shape((rows, width), BF16),),
            in_specs=[VMEM] * (1 + len(got) + len(parts)) + [ANY] * len(wait),
            out_specs=(VMEM,) * (n_z + 1),
            compiler_params=params(8),
            cost_estimate=cost(4 * own.size, 10 * own.size),
        )(own, *got, *parts, *wait)

    def adam(own, got, moment_one, moment_two, step_count, wait):
        def kernel(step_ref, own_ref, *refs):
            got_refs, (m1, m2) = refs[: len(got)], refs[len(got) : len(got) + 2]
            first_ref, second_ref, low_ref = refs[-3:]
            projected = own_ref[...]
            for ref in got_refs:
                projected = projected + ref[...].astype(F32)
            first = 0.9 * m1[...] + 0.1 * projected
            second = 0.999 * m2[...] + 0.001 * projected * projected
            first_ref[...] = first
            second_ref[...] = second
            count = step_ref[0]
            ones = jnp.ones(first.shape, F32)
            first_hat = first / ((1.0 - power(0.9, count)) * ones)
            second_hat = second / ((1.0 - power(0.999, count)) * ones)
            low_ref[...] = (first_hat / (jnp.sqrt(second_hat) + 1e-08)).astype(BF16)

        dims = own.shape
        return pl.pallas_call(
            kernel,
            out_shape=(
                shape(dims, F32),
                shape(dims, F32),
                shape(dims, BF16),
            ),
            in_specs=[SMEM] + [VMEM] * (3 + len(got)) + [ANY] * len(wait),
            out_specs=(VMEM,) * 3,
            compiler_params=params(4),
            cost_estimate=cost(20 * own.size, 24 * own.size),
        )(step_count, own, *got, moment_one, moment_two, *wait)

    def step_product(projector, rows, blocks, wait, begin, count, into=None):
        rank = projector.shape[1]
        own = blocks[0][3].shape[1]
        span = 2 * n_y * own
        width = groups * span

        def kernel(p_ref, *refs):
            columns, refs = refs[: len(blocks)], refs[len(blocks) + len(wait) + (into is not None) :]
            out_hbm, done_ref, low, out, sems = refs
            done_ref[...] = jnp.zeros_like(done_ref)
            z, x, c, y = place()
            for (dc, dx, dy, _), ref in zip(blocks, columns):
                tc, tx, ty = (c + dc) % 2, (x + dx) % 2, (y + n_y - dy) % n_y
                for dz in range(n_z):
                    tz = (z + n_z - dz) % n_z
                    row = pl.multiple_of((tc * n_y + ty) * own, own)
                    low[tz * 2 + tx, pl.ds(row, own), :] = ref[dz]
            copies = []
            for k in range(count):
                out[k] = 0.25 * lax.dot_general(
                    p_ref[pl.ds(pl.multiple_of(y * rows, 16), rows), :],
                    low[begin + k],
                    (((1,), (1,)), ((), ())),
                    preferred_element_type=F32,
                )
                copies.append(
                    pltpu.make_async_copy(out.at[k], out_hbm.at[:, pl.ds((begin + k) * span, span)], sems.at[k])
                )
                copies[-1].start()
            for copy in copies:
                copy.wait()

        return pl.pallas_call(
            kernel,
            out_shape=(shape((rows, width), F32), shape((8, 128), F32)),
            in_specs=[VMEM] * (1 + len(blocks))
            + [ANY] * len(wait)
            + [HBM] * (into is not None),
            out_specs=(HBM, VMEM),
            input_output_aliases={} if into is None else {1 + len(blocks) + len(wait): 0},
            scratch_shapes=[
                pltpu.VMEM((groups, span, rank), BF16),
                pltpu.VMEM((count, rows, span), F32),
                pltpu.SemaphoreType.DMA((count,)),
            ],
            compiler_params=params(16),
            cost_estimate=cost(2 * rows * rank * width, 4 * rows * width),
        )(projector, *[block[3] for block in blocks], *wait, *([] if into is None else [into]))

    def own_product(cotangent, weight, begin, chunks, into, *wait):
        tokens, width = cotangent.shape
        rows = weight.shape[0]
        step = 256
        operands = [cotangent, weight] + ([] if into is None else [into])

        def kernel(g, w_hbm, *refs):
            out_hbm, done_ref, w, out, sems = refs[-5:]
            y = lax.axis_index("fsdp")
            copies = []
            for k in range(chunks):
                span = pl.ds((begin + k) * step, step)
                copies.append(pltpu.make_async_copy(w_hbm.at[span, :], w.at[k], sems.at[k]))
                copies[-1].start()
            done_ref[...] = jnp.zeros_like(done_ref)
            outs = []
            for k in range(chunks):
                copies[k].wait()
                out[k] = lax.dot_general(
                    g[...], w[k], (((1,), (1,)), ((), ())), preferred_element_type=F32
                ).astype(BF16)
                column = pl.multiple_of(y * rows + (begin + k) * step, step)
                outs.append(
                    pltpu.make_async_copy(
                        out.at[k], out_hbm.at[:, pl.ds(column, step)], sems.at[chunks + k]
                    )
                )
                outs[-1].start()
            for copy in outs:
                copy.wait()

        return pl.pallas_call(
            kernel,
            out_shape=(shape((tokens, rows * n_y), BF16), shape((8, 128), F32)),
            in_specs=[VMEM] + [HBM] * (len(operands) - 1) + [ANY] * len(wait),
            out_specs=(HBM, VMEM),
            input_output_aliases={} if into is None else {2: 0},
            scratch_shapes=[
                pltpu.VMEM((chunks, step, width), BF16),
                pltpu.VMEM((chunks, tokens, step), BF16),
                pltpu.SemaphoreType.DMA((2 * chunks,)),
            ],
            compiler_params=params(10),
            cost_estimate=cost(2 * tokens * rows * width, 2 * (tokens + rows) * width),
        )(*operands, *wait)

    def stack(values, pieces):
        rows, width = sum(piece.shape[0] for piece in pieces), pieces[0].shape[1]

        def kernel(*refs):
            out_ref, piece_ref = refs[-2:]
            for k in range(len(values)):
                out_ref[k] = refs[k][...]
            begin = 0
            for k, piece in enumerate(pieces):
                piece_ref[begin : begin + piece.shape[0], :] = refs[len(values) + k][...]
                begin += piece.shape[0]

        return pl.pallas_call(
            kernel,
            out_shape=(
                shape((len(values),) + values[0].shape, values[0].dtype),
                shape((rows, width), pieces[0].dtype),
            ),
            in_specs=[VMEM] * (len(values) + len(pieces)),
            out_specs=(VMEM, VMEM),
            compiler_params=params(4),
            cost_estimate=cost(0, 0),
        )(*values, *pieces)

    def relay(value, wait, sizes=None):
        counts = sizes or (value.shape[0],)

        def kernel(ref, *refs):
            outs, begin = refs[len(wait) :], 0
            for count, out_ref in zip(counts, outs):
                out_ref[...] = ref[begin : begin + count]
                begin += count

        copies = pl.pallas_call(
            kernel,
            out_shape=tuple(shape((count,) + value.shape[1:], value.dtype) for count in counts),
            in_specs=[VMEM] + [ANY] * len(wait),
            out_specs=(VMEM,) * len(counts),
            compiler_params=params(4),
            cost_estimate=cost(0, 2 * value.size),
        )(value, *wait)
        return copies if sizes else copies[0]

    def other_product(cotangent, pieces, into):
        tokens, width = cotangent.shape
        rows = sum(piece[3] for piece in pieces)
        step = 256 if rows % 256 == 0 else 128
        chunks = rows // step

        def kernel(g_ref, *refs):
            w_refs = refs[: len(pieces)]
            out_hbm, w, out, sems = refs[-4:]
            z, x, c, y = place()
            copies = []
            for k, ((first, _, offset, count), ref) in enumerate(zip(pieces, w_refs)):
                row = pl.multiple_of(first(z, x, c), 16)
                copies.append(
                    pltpu.make_async_copy(
                        ref.at[pl.ds(offset, count)], w.at[pl.ds(row, count)], sems.at[k]
                    )
                )
                copies[-1].start()
            for copy in copies:
                copy.wait()
            outs = []
            for k in range(chunks):
                out[k] = lax.dot_general(
                    g_ref[...],
                    w[pl.ds(k * step, step), :],
                    (((1,), (1,)), ((), ())),
                    preferred_element_type=F32,
                ).astype(BF16)
                column = pl.multiple_of((1 - y) * rows + k * step, step)
                outs.append(
                    pltpu.make_async_copy(
                        out.at[k], out_hbm.at[:, pl.ds(column, step)], sems.at[len(pieces) + k]
                    )
                )
                outs[-1].start()
            for copy in outs:
                copy.wait()

        return pl.pallas_call(
            kernel,
            out_shape=shape(into.shape, BF16),
            in_specs=[VMEM] + [ANY] * len(pieces) + [HBM],
            out_specs=HBM,
            input_output_aliases={1 + len(pieces): 0},
            scratch_shapes=[
                pltpu.VMEM((rows, width), BF16),
                pltpu.VMEM((chunks, tokens, step), BF16),
                pltpu.SemaphoreType.DMA((len(pieces) + chunks,)),
            ],
            compiler_params=params(8),
            cost_estimate=cost(2 * tokens * rows * width, 2 * (tokens + rows) * width),
        )(cotangent, *[piece[1] for piece in pieces], into)

    def on_device(attn, cotangent, weight, projector, moment_one, moment_two, step_count):
        shard_rows, width = weight.shape
        own_rows = moment_one.shape[0]
        if n_y != 2 or own_rows % 16 or shard_rows % 768 or n_z % 2:
            return plain(attn, cotangent, weight, projector, moment_one, moment_two, step_count)
        eighth = shard_rows // 8
        first, second, own_projector = cut(weight, projector)
        over_y = [to_plane(first, 0, 1)]
        outgoing, keep = local_sums(attn, own_projector, cotangent)
        over_y.append(to_plane(relay(second, [over_y[0]]), 0, 1))
        sums = core_sum(keep, to_core(relay(outgoing, [over_y[0]])))
        over_z = to_z_pair(over_y[0])
        got = [to_plane(part, dx, dy) for (dx, dy), part in zip(plane, sums[1:])]
        grad_input, done = own_product(
            cotangent, weight, 0, shard_rows // 256, None, sums[1]
        )
        over_y[1] = relay(over_y[1], [done])
        sums = plane_sum(sums[0], got, over_y, [done, over_z])
        own = sums[n_z]

        over_x = to_plane(own, 1, 0)
        got = [to_z(part, dz) for dz, part in zip(range(1, n_z), sums[1:n_z])]
        first_moment, second_moment, low_step = adam(
            sums[0], got, moment_one, moment_two, step_count, []
        )
        column, rest = stack(
            [low_step] + [to_z(low_step, dz) for dz in range(1, n_z)], [over_x, over_y[1]]
        )
        rest = to_z_pair(rest)

        blocks = [(0, 0, 0, column), (1, 0, 0, to_core(column))]
        for dx, dy in plane:
            got = to_plane(column, dx, dy)
            blocks += [(0, dx, dy, got), (1, dx, dy, to_core(got))]
        half = eighth // 2
        other = [to_core(part) for part in (own, over_x, over_z)]
        weight_step, done = step_product(
            own_projector, shard_rows, blocks, other[:2], 0, groups // 2
        )
        late = relay(rest, [done])
        weight_step, done = step_product(
            own_projector, shard_rows, blocks, [late], groups // 2, groups // 2, weight_step
        )
        pieces = []
        for part, twin, held in (
            (own, other[0], [(0, 0, 0, eighth)]),
            (over_x, other[1], [(1, 0, 0, eighth)]),
            (over_z, other[2], [(0, 1, 0, half)]),
            (rest, to_core(late), [(1, 1, 0, eighth), (0, 1, half, eighth - half)]),
        ):
            for dc, array in enumerate((part, twin)):
                offset = 0
                for dx, dz, begin, count in held:
                    row = lambda z, x, c, dx=dx, dz=dz, dc=dc, begin=begin: (
                        (((x + dx) % 2) * 2 + (z + dz) % 2) * 2 + (c + dc) % 2
                    ) * eighth + begin
                    pieces.append((row, array, offset, count))
                    offset += count
        grad_input = other_product(cotangent, pieces, grad_input)
        return grad_input, weight_step, first_moment, second_moment

    rows = P(("dp", "fsdp"), None)
    return jax.shard_map(
        on_device,
        mesh=mesh,
        in_specs=(rows, rows, P("fsdp", None), P(), rows, rows, P()),
        out_specs=(rows, P("fsdp", None), rows, rows),
        check_vma=False,
    )
```
